32 devices in a mesh: shot: 4 (over z), space: 8 (over y, x, core).
Axes of the slice: x: 2, y: 2, z: 4, core: 2. Of those that a mesh axis runs over, the one named last changes fastest.
Arguments:
- courant: float32 [64, 64, 256], P('space'), may hold values from 0.2 to 0.45
- field_old: float32 [4, 64, 64, 256], P('shot', 'space'), may hold values from -0.9 to 0.9
- field_now: float32 [4, 64, 64, 256], P('shot', 'space'), may hold values from -0.9 to 0.9
- adjoint_late: float32 [4, 64, 64, 256], P('shot', 'space'), may hold values from -0.9 to 0.9
- adjoint_now: float32 [4, 64, 64, 256], P('shot', 'space'), may hold values from -0.9 to 0.9
- source_x: int32 [4], P('shot'), may hold values from 0 to 63
- source_yz: int32 [4], P('shot'), may hold values from 0 to 16383
- wavelet: float32 [4, 2], P('shot'), may hold values from -18 to 18
- receiver_x: int32 [4, 256], P('shot'), may hold values from 0 to 63
- receiver_yz: int32 [4, 256], P('shot'), may hold values from 0 to 16383
- residual_trace: float32 [4, 256, 2], P('shot'), may hold values from -18 to 18
Outputs:
- speed_gradient: float32 [64, 64, 256], P('space', 'shot')
The draws below stay inside these ranges and needn't reach their ends.
All inputs are finite; a program needn't handle non-finite values.
Results may differ from the reference program's by a relative error of at most 0.00002.
Values sent between devices are 32-bit elements; how exact they have to be, the bound alone decides.
No kernel may reach another device: no remote copies, remote signals or barrier semaphores. Data moves between devices by JAX's collectives and lax.ppermute only.
A program may use at most 64 MiB of HBM per device.

```python
import jax
import jax.numpy as jnp

NY = 64
NZ = 256
RECV = 256
SHOTS = 4
NX = 64


def plant(entries, own_key, smallest, top_value):
    longest = entries.shape.index(max(entries.shape))
    spots = []
    for shift in (0, 1):
        where = [jax.random.randint(jax.random.fold_in(own_key, axis), (), 0, length) for axis, length in enumerate(entries.shape)]
        where[longest] = (where[longest] + shift) % entries.shape[longest]
        spots.append(tuple(where))
    return entries.at[spots[0]].set(smallest).at[spots[1]].set(top_value)


def block_scale(key, extent, pieces, least, largest):
    def one(dim, parts):
        draws = jax.random.uniform(jax.random.fold_in(jax.random.fold_in(key, 6), dim), (parts,), jnp.float32, least / len(pieces), largest / len(pieces))
        return jnp.repeat(jnp.exp(draws), extent[dim] // parts).reshape((-1,) + (1,) * (len(extent) - dim - 1))

    level = one(*pieces[0])
    for cut in pieces[1:]:
        level = level * one(*cut)
    return level


def normal_values(own_key, extent, width, limit, shards=(), dtype=jnp.bfloat16):
    drawn = width * jax.random.normal(own_key, extent, jnp.float32)
    if shards:
        drawn = drawn * block_scale(own_key, extent, shards, -0.22, 0.18)
    return jnp.clip(drawn, -limit, limit).astype(dtype)


def setup_inputs(seed: int = 0) -> dict:
    key_list = jax.random.split(jax.random.key(seed), 12)
    courant = jnp.clip(0.2 + 0.24999999 * jax.random.uniform(key_list[0], (NX, NY, NZ), jnp.float32) ** block_scale(key_list[0], (NX, NY, NZ), ((0, 8),), -0.2, 0.2), 0.2, 0.45)
    field_old = normal_values(key_list[1], (SHOTS, NX, NY, NZ), 0.15, 0.9, ((0, 4), (1, 8)), jnp.float32)
    field_now = normal_values(key_list[2], (SHOTS, NX, NY, NZ), 0.15, 0.9, ((0, 4), (1, 8)), jnp.float32)
    adjoint_late = normal_values(key_list[3], (SHOTS, NX, NY, NZ), 0.15, 0.9, ((0, 4), (1, 8)), jnp.float32)
    adjoint_now = normal_values(key_list[4], (SHOTS, NX, NY, NZ), 0.15, 0.9, ((0, 4), (1, 8)), jnp.float32)
    source_x = plant(jax.random.randint(key_list[5], (SHOTS,), 0, NX), jax.random.fold_in(key_list[5], 1), 0, NX - 1).astype(jnp.int32)
    source_yz = plant(jax.random.randint(key_list[6], (SHOTS,), 0, NY * NZ), jax.random.fold_in(key_list[6], 1), 0, (NY * NZ) - 1).astype(jnp.int32)
    wavelet = normal_values(key_list[7], (SHOTS, 2), 3.0, 18.0, ((0, 4),), jnp.float32)
    receiver_x = plant(jax.random.randint(key_list[8], (SHOTS, RECV), 0, NX), jax.random.fold_in(key_list[8], 1), 0, NX - 1).astype(jnp.int32)
    receiver_yz = plant(jax.random.randint(key_list[9], (SHOTS, RECV), 0, NY * NZ), jax.random.fold_in(key_list[9], 1), 0, (NY * NZ) - 1).astype(jnp.int32)
    residual_trace = normal_values(key_list[10], (SHOTS, RECV, 2), 3.0, 18.0, ((0, 4),), jnp.float32)
    return dict(courant=courant, field_old=field_old, field_now=field_now, adjoint_late=adjoint_late, adjoint_now=adjoint_now, source_x=source_x, source_yz=source_yz, wavelet=wavelet, receiver_x=receiver_x, receiver_yz=receiver_yz, residual_trace=residual_trace)


STENCIL_MIDDLE = -205.0 / 72.0
STENCIL_SIDE = (8.0 / 5.0, -1.0 / 5.0, 8.0 / 315.0, -1.0 / 560.0)


def laplace(wavefield):
    size_x, size_y, size_z = wavefield.shape
    padded = jnp.pad(wavefield, 4)

    def window(shift_x, shift_y, shift_z):
        return padded[4 + shift_x:4 + shift_x + size_x, 4 + shift_y:4 + shift_y + size_y, 4 + shift_z:4 + shift_z + size_z]

    summed = 3.0 * STENCIL_MIDDLE * window(0, 0, 0)
    for offset in range(1, 5):
        weight = STENCIL_SIDE[offset - 1]
        summed = summed + weight * (window(offset, 0, 0) + window(-offset, 0, 0) + window(0, offset, 0) + window(0, -offset, 0) + window(0, 0, offset) + window(0, 0, -offset))
    return summed


def inject(wavefield, cells_x, cells_yz, amounts):
    flattened = wavefield.reshape(wavefield.shape[0], -1)
    flattened = flattened.at[cells_x, cells_yz].add(amounts)
    return flattened.reshape(wavefield.shape)


def reference(courant, field_old, field_now, adjoint_late, adjoint_now, source_x, source_yz, wavelet, receiver_x, receiver_yz, residual_trace):
    speed_sq = courant * courant
    gradient_sum = jnp.zeros(courant.shape, jnp.float32)
    for shot_id in range(SHOTS):
        accel_one = inject(laplace(field_now[shot_id]), source_x[shot_id], source_yz[shot_id], wavelet[shot_id, 0])
        field_mid = 2.0 * field_now[shot_id] - field_old[shot_id] + speed_sq * accel_one
        accel_two = inject(laplace(field_mid), source_x[shot_id], source_yz[shot_id], wavelet[shot_id, 1])
        adjoint_mid = 2.0 * adjoint_now[shot_id] - adjoint_late[shot_id] + laplace(speed_sq * adjoint_now[shot_id])
        adjoint_mid = inject(adjoint_mid, receiver_x[shot_id], receiver_yz[shot_id], residual_trace[shot_id, :, 0])
        adjoint_early = 2.0 * adjoint_mid - adjoint_now[shot_id] + laplace(speed_sq * adjoint_mid)
        adjoint_early = inject(adjoint_early, receiver_x[shot_id], receiver_yz[shot_id], residual_trace[shot_id, :, 1])
        gradient_sum = gradient_sum + 2.0 * courant * (adjoint_early * accel_one + adjoint_mid * accel_two)
    return gradient_sum
```

```python
import functools
import jax
import jax.numpy as jnp
from jax import lax
from jax.experimental import pallas as pl
from jax.experimental.pallas import tpu as pltpu
from jax.sharding import PartitionSpec as P

MIDDLE = 3.0 * (-205.0 / 72.0)
SIDE = (8.0 / 5.0, -1.0 / 5.0, 8.0 / 315.0, -1.0 / 560.0)
REACH = 4
F32 = jnp.float32
BF16 = jnp.bfloat16
VMEM_LIMIT = 48 * 1024 * 1024


def placed(layer, odd, slab):
    return layer + odd * (slab - 1 - 2 * layer)


def grids(size_y, size_z):
    rows = lax.broadcasted_iota(jnp.int32, (size_y, size_z), 0)
    columns = lax.broadcasted_iota(jnp.int32, (size_y, size_z), 1)
    return rows, columns


def own_laplace(layers, at, slab, rows, columns):
    centre = layers[at]
    size_y, size_z = centre.shape
    total = MIDDLE * centre
    for offset in range(1, REACH + 1):
        near = jnp.where(rows >= offset, pltpu.roll(centre, offset, 0), 0.0)
        near += jnp.where(rows < size_y - offset, pltpu.roll(centre, size_y - offset, 0), 0.0)
        near += jnp.where(columns >= offset, pltpu.roll(centre, offset, 1), 0.0)
        near += jnp.where(columns < size_z - offset, pltpu.roll(centre, size_z - offset, 1), 0.0)
        if at - offset >= 0:
            near += layers[at - offset]
        if at + offset < slab:
            near += layers[at + offset]
        total += SIDE[offset - 1] * near
    return total


def across(depth, layers):
    total = None
    for beyond in range(REACH - depth):
        term = SIDE[depth + beyond] * layers(beyond)
        total = term if total is None else total + term
    return total


def early_kernel(slab, courant, now, adjoint, packet, c_part, n_part, a_part, sems):
    odd = lax.rem(lax.axis_index("space"), 2)
    start = odd * (slab - REACH)
    copies = [
        pltpu.make_async_copy(source.at[pl.ds(start, REACH)], target, sems.at[number])
        for number, (source, target) in enumerate(
            ((courant, c_part), (now, n_part), (adjoint, a_part))
        )
    ]
    for copy in copies:
        copy.start()
    for copy in copies:
        copy.wait()
    for layer in range(REACH):
        at = placed(layer, odd, REACH)
        packet[layer] = n_part[at]
        speed = c_part[at]
        packet[REACH + layer] = speed * speed * a_part[at]


def local_kernel(
    slab,
    source_x,
    source_yz,
    wavelet,
    courant,
    old,
    now,
    late,
    adjoint,
    receiver_x,
    receiver_yz,
    residual,
    accel_one,
    field_mid,
    adjoint_mid,
    early_rest,
    packet_in,
    packet_out,
    scaled,
    marks,
    added,
):
    space = lax.axis_index("space")
    odd = lax.rem(space, 2)
    first_x = space * slab
    size_y, size_z = courant.shape[1:]
    z_bits = size_z.bit_length() - 1
    rows, columns = grids(size_y, size_z)

    local_x = receiver_x[...] - first_x
    cells = receiver_yz[...]
    inside = (local_x >= 0) & (local_x < slab)
    wanted = jnp.where(inside, local_x * size_y + jnp.right_shift(cells, z_bits), -1)
    count = wanted.shape[1]
    line = lax.broadcasted_iota(jnp.int32, (slab * size_y, count), 0)
    marks[...] = jnp.where(line == wanted, 1.0, 0.0).astype(BF16)
    depth = lax.broadcasted_iota(jnp.int32, (size_z, count), 0)
    hit = depth == jnp.bitwise_and(cells, size_z - 1)
    for step in range(2):
        rest = residual[pl.ds(step, 1), :]
        total = None
        for _ in range(3):
            part = rest.astype(BF16).astype(F32)
            rest = rest - part
            spread = jnp.where(hit, part, 0.0).astype(BF16)
            term = lax.dot_general(
                marks[...], spread, (((1,), (1,)), ((), ())), preferred_element_type=F32
            )
            total = term if total is None else total + term
        added[step] = total

    for at in range(slab):
        scaled[at] = courant[at] * courant[at] * adjoint[at]
    cell = rows * size_z + columns
    source_layer = source_x[0] - first_x
    for at in range(slab):
        to = placed(at, odd, slab)
        speed_sq = courant[at] * courant[at]
        spot = jnp.where(source_layer == at, source_yz[0], -1)
        laplace = own_laplace(now, at, slab, rows, columns)
        laplace += jnp.where(cell == spot, wavelet[0, 0], 0.0)
        accel_one[to] = laplace
        field_mid[to] = 2.0 * now[at] - old[at] + speed_sq * laplace
        mine = pl.ds(at * size_y, size_y)
        adjoint_mid[to] = (
            2.0 * adjoint[at]
            - late[at]
            + own_laplace(scaled, at, slab, rows, columns)
            + added[0, mine, :]
        )
        early_rest[to] = added[1, mine, :] - adjoint[at]
    for layer in range(REACH):
        inner = slab - 1 - layer
        at = placed(inner, odd, slab)
        speed = courant[at]
        packet_in[layer] = now[at]
        packet_in[REACH + layer] = scaled[at]
        packet_in[2 * REACH + layer] = speed
        packet_in[3 * REACH + layer] = field_mid[inner]
        packet_in[4 * REACH + layer] = speed * speed * adjoint_mid[inner]
        speed = courant[placed(layer, odd, slab)]
        packet_out[layer] = speed
        packet_out[REACH + layer] = field_mid[layer]
        packet_out[2 * REACH + layer] = speed * speed * adjoint_mid[layer]


def finished_halo(speeds, partial, own):
    return [
        partial(layer) + speeds(layer) * speeds(layer) * across(layer, own)
        for layer in range(REACH)
    ]


def scatter_rows(gradient, outputs, shots):
    rows = gradient.shape[1] // shots
    me = lax.axis_index("shot")
    for shift in range(shots):
        first = pl.multiple_of(lax.rem(me + shift, shots) * rows, rows)
        outputs[shift][...] = gradient[:, pl.ds(first, rows), :]


def inner_kernel(
    slab,
    shots,
    source_x,
    source_yz,
    wavelet,
    courant,
    accel_one,
    field_mid,
    adjoint_mid,
    early_rest,
    own_in,
    halo_in,
    halo_early,
    *rest,
):
    outer, outputs = rest[0], rest[1 : 1 + shots]
    accel, adjoint, mid, scaled, next_mid, next_scaled, gradient = rest[1 + shots :]
    space = lax.axis_index("space")
    odd = lax.rem(space, 2)
    size_y, size_z = courant.shape[1:]
    rows, columns = grids(size_y, size_z)

    for layer in range(REACH):
        speed = halo_in[2 * REACH + layer]
        speed_sq = speed * speed
        next_mid[layer] = halo_in[3 * REACH + layer] + speed_sq * across(
            layer, lambda beyond: own_in[beyond]
        )
        next_scaled[layer] = halo_in[4 * REACH + layer] + speed_sq * across(
            layer, lambda beyond: own_in[REACH + beyond]
        )

    def beyond_faces(at, out_layers, in_layers):
        total = None
        if at < REACH:
            total = across(at, out_layers)
        if slab - 1 - at < REACH:
            other = across(slab - 1 - at, in_layers)
            total = other if total is None else total + other
        return total

    for at in range(slab):
        speed = courant[placed(at, odd, slab)]
        speed_sq = speed * speed
        extra = beyond_faces(
            at, lambda beyond: halo_early[beyond], lambda beyond: halo_in[beyond]
        )
        accel[at] = accel_one[at] if extra is None else accel_one[at] + extra
        mid[at] = field_mid[at] if extra is None else field_mid[at] + speed_sq * extra
        extra = beyond_faces(
            at, lambda beyond: halo_early[REACH + beyond], lambda beyond: halo_in[REACH + beyond]
        )
        adjoint[at] = adjoint_mid[at] if extra is None else adjoint_mid[at] + extra
        scaled[at] = speed_sq * adjoint[at]

    cell = rows * size_z + columns
    source_layer = placed(source_x[0] - space * slab, odd, slab)
    for at in range(slab):
        spot = jnp.where(source_layer == at, source_yz[0], -1)
        accel_two = own_laplace(mid, at, slab, rows, columns)
        accel_two += jnp.where(cell == spot, wavelet[0, 1], 0.0)
        early = 2.0 * adjoint[at] + early_rest[at]
        early += own_laplace(scaled, at, slab, rows, columns)
        depth = slab - 1 - at
        if depth < REACH:
            accel_two += across(depth, lambda beyond: next_mid[beyond])
            early += across(depth, lambda beyond: next_scaled[beyond])
        if at < REACH:
            outer[at] = accel[at]
            outer[REACH + at] = adjoint[at]
            outer[2 * REACH + at] = accel_two
            outer[3 * REACH + at] = early
        else:
            speed = courant[placed(at, odd, slab)]
            gradient[at - REACH] = (
                2.0 * speed * (early * accel[at] + adjoint[at] * accel_two)
            )
    scatter_rows(gradient, outputs, shots)


def outer_kernel(slab, shots, courant, outer, own_early, halo_late, *rest):
    outputs, (next_mid, next_scaled, gradient) = rest[:shots], rest[shots:]
    odd = lax.rem(lax.axis_index("space"), 2)
    for layer in range(REACH):
        speed = halo_late[layer]
        speed_sq = speed * speed
        next_mid[layer] = halo_late[REACH + layer] + speed_sq * across(
            layer, lambda beyond: own_early[beyond]
        )
        next_scaled[layer] = halo_late[2 * REACH + layer] + speed_sq * across(
            layer, lambda beyond: own_early[REACH + beyond]
        )
    for at in range(REACH):
        accel_two = outer[2 * REACH + at] + across(at, lambda beyond: next_mid[beyond])
        early = outer[3 * REACH + at] + across(at, lambda beyond: next_scaled[beyond])
        speed = courant[placed(at, odd, slab)]
        gradient[at] = 2.0 * speed * (early * outer[at] + outer[REACH + at] * accel_two)
    scatter_rows(gradient, outputs, shots)


def sum_kernel(slab, shots, *refs):
    outers, inners, out = refs[:shots], refs[shots : 2 * shots], refs[2 * shots]
    odd = lax.rem(lax.axis_index("space"), 2)
    for at in range(slab):
        parts = [ref[at] for ref in outers] if at < REACH else [ref[at - REACH] for ref in inners]
        out[placed(at, odd, slab)] = functools.reduce(lambda a, b: a + b, parts)


def call(kernel, shapes, in_spaces, scratch, flops, moved):
    many = isinstance(shapes, list)
    return pl.pallas_call(
        kernel,
        out_shape=[jax.ShapeDtypeStruct(s, F32) for s in shapes]
        if many
        else jax.ShapeDtypeStruct(shapes, F32),
        in_specs=[pl.BlockSpec(memory_space=space) for space in in_spaces],
        out_specs=[pl.BlockSpec(memory_space=pltpu.VMEM) for _ in shapes]
        if many
        else pl.BlockSpec(memory_space=pltpu.VMEM),
        scratch_shapes=scratch,
        compiler_params=pltpu.CompilerParams(vmem_limit_bytes=VMEM_LIMIT),
        cost_estimate=pl.CostEstimate(flops=flops, bytes_accessed=moved, transcendentals=0),
    )


def on_device(
    courant,
    field_old,
    field_now,
    adjoint_late,
    adjoint_now,
    source_x,
    source_yz,
    wavelet,
    receiver_x,
    receiver_yz,
    residual_trace,
):
    slab, size_y, size_z = courant.shape
    shots = lax.axis_size("shot")
    devices = lax.axis_size("space")
    plane = (size_y, size_z)
    layer_bytes = 4 * size_y * size_z
    inner_layers = slab - REACH
    part_rows = size_y // shots
    V, S, A = pltpu.VMEM, pltpu.SMEM, pl.ANY
    out_pairs = [(i, i + 1) for i in range(1, devices - 1, 2)]
    out_pairs += [(b, a) for a, b in out_pairs]
    in_pairs = [(i, i ^ 1) for i in range(devices)]
    old, now, late, adjoint = (
        field[0] for field in (field_old, field_now, adjoint_late, adjoint_now)
    )
    residual = residual_trace[0].T

    own_early = call(
        functools.partial(early_kernel, slab),
        (2 * REACH,) + plane,
        [A, A, A],
        [pltpu.VMEM((REACH,) + plane, F32)] * 3 + [pltpu.SemaphoreType.DMA((3,))],
        3 * REACH * size_y * size_z,
        20 * layer_bytes,
    )(courant, now, adjoint)
    halo_early = lax.ppermute(own_early, "space", out_pairs)

    whole = (slab,) + plane
    accel_one, field_mid, adjoint_mid, early_rest, own_in, own_late = call(
        functools.partial(local_kernel, slab),
        [whole] * 4 + [(5 * REACH,) + plane, (3 * REACH,) + plane],
        [S, S, S, V, V, V, V, V, V, V, V],
        [
            pltpu.VMEM(whole, F32),
            pltpu.VMEM((slab * size_y, receiver_x.shape[1]), BF16),
            pltpu.VMEM((2, slab * size_y, size_z), F32),
        ],
        100 * slab * size_y * size_z,
        13 * slab * layer_bytes,
    )(
        source_x,
        source_yz,
        wavelet,
        courant,
        old,
        now,
        late,
        adjoint,
        receiver_x,
        receiver_yz,
        residual,
    )
    halo_in = lax.ppermute(own_in, "space", in_pairs)
    halo_late = lax.ppermute(own_late, "space", out_pairs)

    outer, *inner_parts = call(
        functools.partial(inner_kernel, slab, shots),
        [(4 * REACH,) + plane] + [(inner_layers, part_rows, size_z)] * shots,
        [S, S, S, V, V, V, V, V, V, V, V],
        [
            pltpu.VMEM(whole, F32),
            pltpu.VMEM(whole, F32),
            pltpu.VMEM(whole, F32),
            pltpu.VMEM(whole, F32),
            pltpu.VMEM((REACH,) + plane, F32),
            pltpu.VMEM((REACH,) + plane, F32),
            pltpu.VMEM((inner_layers,) + plane, F32),
        ],
        100 * slab * size_y * size_z,
        13 * slab * layer_bytes,
    )(
        source_x,
        source_yz,
        wavelet,
        courant,
        accel_one,
        field_mid,
        adjoint_mid,
        early_rest,
        own_in,
        halo_in,
        halo_early,
    )
    shifts = [[(i, (i + k) % shots) for i in range(shots)] for k in range(shots)]
    inner_parts = inner_parts[:1] + [
        lax.ppermute(inner_parts[k], "shot", shifts[k]) for k in range(1, shots)
    ]
    outer_parts = call(
        functools.partial(outer_kernel, slab, shots),
        [(REACH, part_rows, size_z)] * shots,
        [V, V, V, V],
        [
            pltpu.VMEM((REACH,) + plane, F32),
            pltpu.VMEM((REACH,) + plane, F32),
            pltpu.VMEM((REACH,) + plane, F32),
        ],
        50 * REACH * size_y * size_z,
        48 * layer_bytes,
    )(courant, outer, own_early, halo_late)
    outer_parts = list(outer_parts[:1]) + [
        lax.ppermute(outer_parts[k], "shot", shifts[k]) for k in range(1, shots)
    ]
    return call(
        functools.partial(sum_kernel, slab, shots),
        (slab, part_rows, size_z),
        [V] * (2 * shots),
        [],
        slab * size_y * size_z,
        2 * slab * layer_bytes,
    )(*outer_parts, *inner_parts)


def solution(mesh):
    field = P("shot", "space", None, None)
    specs = (
        P("space", None, None),
        field,
        field,
        field,
        field,
        P("shot"),
        P("shot"),
        P("shot", None),
        P("shot", None),
        P("shot", None),
        P("shot", None, None),
    )
    return jax.shard_map(
        on_device, mesh=mesh, in_specs=specs, out_specs=P("space", "shot", None), check_vma=False
    )
```

```python
import functools
import jax
import jax.numpy as jnp
from jax import lax
from jax.experimental import pallas as pl
from jax.experimental.pallas import tpu as pltpu
from jax.sharding import PartitionSpec as P

MIDDLE = 3.0 * (-205.0 / 72.0)
SIDE = (8.0 / 5.0, -1.0 / 5.0, 8.0 / 315.0, -1.0 / 560.0)
REACH = 4
F32 = jnp.float32
BF16 = jnp.bfloat16
VMEM_LIMIT = 32 * 1024 * 1024
SMALL, LARGE = 10**6, 10**10


def placed(layer, outward, odd):
    layer = layer if outward else 2 * REACH - 1 - layer
    return layer + odd * (2 * REACH - 1 - 2 * layer)


def grids(size_y, size_z):
    rows = lax.broadcasted_iota(jnp.int32, (size_y, size_z), 0)
    columns = lax.broadcasted_iota(jnp.int32, (size_y, size_z), 1)
    return rows, columns


def three_parts(values):
    high = values.astype(BF16)
    rest = values - high.astype(F32)
    middle = rest.astype(BF16)
    return high, middle, (rest - middle.astype(F32)).astype(BF16)


def exact_dot(left, right):
    def dot(a, b):
        return jnp.dot(left[a], right[b], preferred_element_type=F32)

    return dot(0, 0) + (dot(0, 1) + dot(1, 0)) + (dot(1, 1) + dot(0, 2) + dot(2, 0))


def band(size, block, middle):
    rows, columns = grids(size, size)
    distance = jnp.abs(rows - columns)
    weights = jnp.where(distance == 0, middle, 0.0)
    for offset in range(1, REACH + 1):
        weights = jnp.where(distance == offset, SIDE[offset - 1], weights)
    bits = block.bit_length() - 1
    return jnp.where(jnp.right_shift(rows, bits) == jnp.right_shift(columns, bits), weights, 0.0)


def plane_laplace(layers, along_y, along_z):
    shape = (len(layers),) + layers[0].shape
    parts = three_parts(jnp.concatenate(layers, axis=0))
    return (exact_dot(parts, along_z) + exact_dot(along_y, parts)).reshape(shape)


def weighted(terms):
    total = None
    for distance in range(1, REACH + 1):
        found = [layer() for at, layer in terms if at == distance]
        if found:
            term = SIDE[distance - 1] * functools.reduce(lambda a, b: a + b, found)
            total = term if total is None else total + term
    return total


def within(at, layers):
    return weighted([(abs(at - i), lambda i=i: layers(i)) for i in range(REACH) if i != at])


def from_other(at, layers):
    last = 2 * REACH - 1
    return weighted([(last - i - at, lambda i=i: layers(i)) for i in range(REACH)])


def across(at, layers):
    return weighted([(at + 1 + i, lambda i=i: layers(i)) for i in range(REACH)])


def add(*values):
    return functools.reduce(lambda a, b: a + b, [v for v in values if v is not None])


def early_kernel(courant, now, adjoint, *refs):
    packets, adjoints, sems = refs[:2], refs[2:4], refs[4]
    odd = lax.rem(lax.axis_index("space"), 2)
    copies = []
    for half in range(2):
        for layer in range(REACH):
            at = placed(layer, half == 0, odd)
            for source, target in (
                (courant.at[at], packets[half].at[2 * REACH + layer]),
                (adjoint.at[at], adjoints[half].at[layer]),
                (now.at[at], packets[half].at[layer]),
            ):
                copies.append(pltpu.make_async_copy(source, target, sems.at[len(copies)]))
                copies[-1].start()
    for copy in copies:
        copy.wait()
    for half in range(2):
        for layer in range(REACH):
            speed = packets[half][2 * REACH + layer]
            packets[half][REACH + layer] = speed * speed * adjoints[half][layer]


def half_kernel(outward, mine, other, adjoint_now, old, late, *refs):
    if outward:
        accel, adjoint, packet, bands = refs[:4]
    else:
        bands, accel, adjoint, packet = refs[:4]
    old_half, late_half, sems = refs[4:]
    size_y, size_z = mine.shape[1:]
    odd = lax.rem(lax.axis_index("space"), 2)
    copies = []
    for layer in range(REACH):
        at = placed(layer, outward, odd)
        for source, target in ((old.at[at], old_half), (late.at[at], late_half)):
            copies.append(
                pltpu.make_async_copy(source, target.at[layer], sems.at[len(copies)])
            )
            copies[-1].start()
    if outward:
        along_y = three_parts(band(REACH * size_y, size_y, 0.0))
        along_z = three_parts(band(size_z, size_z, MIDDLE))
        for number in range(3):
            bands[number] = along_y[number]
            bands[3 + number] = along_z[number]
    else:
        along_y, along_z = bands[0:3], bands[3:6]
    flat = [
        plane_laplace([mine[first + at] for at in range(REACH)], along_y, along_z)
        for first in (0, REACH)
    ]
    for copy in copies:
        copy.wait()
    for at in range(REACH):
        speed = mine[2 * REACH + at]
        speed_sq = speed * speed
        laplace = add(
            flat[0][at],
            within(at, lambda i: mine[i]),
            from_other(at, lambda i: other[i]),
        )
        accel[at] = laplace
        packet[at] = 2.0 * mine[at] - old_half[at] + speed_sq * laplace
        laplace = add(
            flat[1][at],
            within(at, lambda i: mine[REACH + i]),
            from_other(at, lambda i: other[REACH + i]),
        )
        field = 2.0 * adjoint_now[at] - late_half[at] + laplace
        adjoint[at] = field
        packet[REACH + at] = speed_sq * field


def next_halo(at, speed, late, own, points):
    speed_sq = speed * speed
    mid = late[at] + speed_sq * (across(at, lambda i: own[i]) + points[at])
    scaled = late[REACH + at] + speed_sq * (
        across(at, lambda i: own[REACH + i]) + points[REACH + at]
    )
    return mid, scaled


def scatter_rows(gradient, outputs, shots):
    rows = gradient.shape[1] // shots
    me = lax.axis_index("shot")
    for shift in range(shots):
        first = pl.multiple_of(jnp.bitwise_xor(me, shift) * rows, rows)
        outputs[shift][...] = gradient[:, pl.ds(first, rows), :]


def inner_kernel(
    pulse,
    receiver_x,
    receiver_yz,
    residual,
    own_in,
    own_out,
    accel_in,
    accel_out,
    adjoint_in,
    adjoint_out,
    late_in,
    late_out,
    now_in,
    now_out,
    bands,
    halo_early,
    halo_late,
    inner,
    outer,
    forward,
    backward,
    points_out,
    marks,
    added,
    points_in,
    mid,
    scaled,
    next_mid,
    next_scaled,
):
    slab = 2 * REACH
    space = lax.axis_index("space")
    odd = lax.rem(space, 2)
    size_y, size_z = own_in.shape[1:]
    along_y, along_z = bands[0:3], bands[3:6]
    z_bits = size_z.bit_length() - 1

    def counted(x):
        local = x - space * slab
        return REACH + local + odd * (slab - 1 - 2 * local)

    cells = receiver_yz[...]
    layer = counted(receiver_x[...])
    inside = (layer >= 0) & (layer < 2 * slab)
    wanted = jnp.where(inside, layer * size_y + jnp.right_shift(cells, z_bits), -1)
    count = wanted.shape[1]
    line = lax.broadcasted_iota(jnp.int32, (2 * slab * size_y, count), 0)
    marks[...] = jnp.where(line == wanted, 1.0, 0.0).astype(BF16)
    depth = lax.broadcasted_iota(jnp.int32, (size_z, count), 0)
    hit = depth == jnp.bitwise_and(cells, size_z - 1)

    def received(step, first, last):
        total = None
        for part in three_parts(residual[pl.ds(step, 1), :]):
            spread = jnp.where(hit, part.astype(F32), 0.0).astype(BF16)
            term = lax.dot_general(
                marks[first * size_y : last * size_y],
                spread,
                (((1,), (1,)), ((), ())),
                preferred_element_type=F32,
            )
            total = term if total is None else total + term
        return total.reshape(last - first, size_y, size_z)

    added[0 : 2 * slab] = received(0, 0, 2 * slab)
    added[2 * slab :] = received(1, REACH, REACH + slab)

    rows, columns = grids(size_y, size_z)
    cell = rows * size_z + columns
    source_layer = counted(pulse[:, 2:3].astype(jnp.int32))
    source_cell = pulse[:, 3:4].astype(jnp.int32)

    def fired(step, at):
        spot = jnp.where(source_layer == at, source_cell, -1)
        return jnp.where(cell == spot, pulse[:, step : step + 1], 0.0)

    for at in range(REACH):
        points_out[at] = fired(0, REACH - 1 - at)
        points_out[REACH + at] = added[REACH - 1 - at]
        points_in[at] = fired(0, REACH + slab + at)
        points_in[REACH + at] = added[REACH + slab + at]
        speed = own_out[2 * REACH + at]
        fire = fired(0, REACH + at)
        outer[at] = accel_out[at] + fire
        outer[REACH + at] = adjoint_out[at] + added[REACH + at]
        outer[2 * REACH + at] = late_out[at] + speed * speed * fire
    for at in range(REACH):
        next_mid[at], next_scaled[at] = next_halo(
            at, halo_early[2 * REACH + at], halo_late, own_in, points_in
        )
    for at in range(REACH):
        to = REACH + slab - 1 - at
        speed = own_in[2 * REACH + at]
        speed_sq = speed * speed
        extra = across(at, lambda i: halo_early[i]) + fired(0, to)
        adjoint = adjoint_in[at] + across(at, lambda i: halo_early[REACH + i]) + added[to]
        inner[at] = accel_in[at] + extra
        inner[REACH + at] = adjoint
        mid[at] = late_in[at] + speed_sq * extra
        scaled[at] = speed_sq * adjoint
    flat_mid = plane_laplace([mid[at] for at in range(REACH)], along_y, along_z)
    flat_scaled = plane_laplace([scaled[at] for at in range(REACH)], along_y, along_z)
    for at in range(REACH):
        to = REACH + at
        forward[at] = add(fired(1, to), from_other(at, lambda i: mid[i]))
        backward[at] = add(
            added[2 * slab + at] - now_out[at],
            from_other(at, lambda i: scaled[i]),
        )
        to = REACH + slab - 1 - at
        forward[REACH + at] = add(
            flat_mid[at],
            fired(1, to),
            within(at, lambda i: mid[i]),
            across(at, lambda i: next_mid[i]),
        )
        backward[REACH + at] = add(
            flat_scaled[at],
            added[2 * slab + slab - 1 - at] - now_in[at],
            2.0 * inner[REACH + at],
            within(at, lambda i: scaled[i]),
            across(at, lambda i: next_scaled[i]),
        )


def middle_kernel(
    shots, own_in, own_out, bands, halo, inner, outer_part, forward, backward, outer, *rest
):
    outputs, (mid, scaled, gradient) = rest[:shots], rest[shots:]
    along_y, along_z = bands[0:3], bands[3:6]
    for at in range(REACH):
        speed = own_out[2 * REACH + at]
        speed_sq = speed * speed
        extra = across(at, lambda i: halo[i])
        adjoint = outer_part[REACH + at] + across(at, lambda i: halo[REACH + i])
        outer[at] = outer_part[at] + extra
        outer[REACH + at] = adjoint
        mid[at] = outer_part[2 * REACH + at] + speed_sq * extra
        scaled[at] = speed_sq * adjoint
    for at in range(REACH):
        ahead = add(forward[REACH + at], from_other(at, lambda i: mid[i]))
        back = add(backward[REACH + at], from_other(at, lambda i: scaled[i]))
        speed = own_in[2 * REACH + at]
        gradient[at] = 2.0 * speed * (back * inner[at] + inner[REACH + at] * ahead)
    scatter_rows(gradient, outputs, shots)
    flat_mid = plane_laplace([mid[at] for at in range(REACH)], along_y, along_z)
    flat_scaled = plane_laplace([scaled[at] for at in range(REACH)], along_y, along_z)
    for at in range(REACH):
        outer[2 * REACH + at] = add(forward[at], flat_mid[at], within(at, lambda i: mid[i]))
        outer[3 * REACH + at] = add(
            backward[at],
            2.0 * outer[REACH + at],
            flat_scaled[at],
            within(at, lambda i: scaled[i]),
        )


def outer_kernel(shots, relayed, own_out, outer, halo_early, points_out, *rest):
    lates, rest = rest[: 1 + relayed], rest[1 + relayed :]
    outputs, (late, next_mid, next_scaled, gradient) = rest[:shots], rest[shots:]
    if relayed:
        for layer in range(2 * REACH):
            late[layer] = lates[0][layer] + lates[1][layer]
    else:
        late = lates[0]
    for at in range(REACH):
        next_mid[at], next_scaled[at] = next_halo(
            at, halo_early[2 * REACH + at], late, own_out, points_out
        )
    for at in range(REACH):
        ahead = outer[2 * REACH + at] + across(at, lambda i: next_mid[i])
        back = outer[3 * REACH + at] + across(at, lambda i: next_scaled[i])
        speed = own_out[2 * REACH + at]
        gradient[at] = 2.0 * speed * (back * outer[at] + outer[REACH + at] * ahead)
    scatter_rows(gradient, outputs, shots)


def add_kernel(*refs):
    refs[-1][...] = functools.reduce(lambda a, b: a + b, [ref[...] for ref in refs[:-1]])


def sum_kernel(inner, *refs):
    outers, out = refs[:-1], refs[-1]
    odd = lax.rem(lax.axis_index("space"), 2)
    for at in range(REACH):
        out[placed(at, True, odd)] = functools.reduce(lambda a, b: a + b, [r[at] for r in outers])
        out[placed(at, False, odd)] = inner[at]


def call(kernel, shapes, in_spaces, scratch, flops, moved):
    def shape(given):
        return jax.ShapeDtypeStruct(given, F32) if isinstance(given, tuple) else given

    many = isinstance(shapes, list)
    return pl.pallas_call(
        kernel,
        out_shape=[shape(s) for s in shapes] if many else shape(shapes),
        in_specs=[pl.BlockSpec(memory_space=space) for space in in_spaces],
        out_specs=[pl.BlockSpec(memory_space=pltpu.VMEM) for _ in shapes]
        if many
        else pl.BlockSpec(memory_space=pltpu.VMEM),
        scratch_shapes=scratch,
        compiler_params=pltpu.CompilerParams(vmem_limit_bytes=VMEM_LIMIT),
        cost_estimate=pl.CostEstimate(flops=flops, bytes_accessed=moved, transcendentals=0),
    )


def both_ways(pairs):
    return pairs + [(b, a) for a, b in pairs]


def on_device(
    courant,
    field_old,
    field_now,
    adjoint_late,
    adjoint_now,
    source_x,
    source_yz,
    wavelet,
    receiver_x,
    receiver_yz,
    residual_trace,
):
    slab, size_y, size_z = courant.shape
    if slab != 2 * REACH:
        raise ValueError("unsupported slab")
    shots = lax.axis_size("shot")
    devices = lax.axis_size("space")
    plane = size_y * size_z
    part_rows = size_y // shots
    V, H = pltpu.VMEM, pltpu.HBM

    def stack(layers):
        return (layers, size_y, size_z)

    def held(layers):
        return pltpu.VMEM(stack(layers), F32)

    def in_hbm(values):
        return pltpu.with_memory_space_constraint(values, pltpu.HBM)

    out_pairs = both_ways([(i, i + 1) for i in range(1, devices - 1, 2)])
    in_pairs = [(i, i ^ 1) for i in range(devices)]
    relayed = devices == 8
    fields = [courant] + [f[0] for f in (adjoint_now, field_now, adjoint_late, field_old)]
    courant, adjoint, now, late, old = [in_hbm(f) for f in fields]
    place = [source_x.astype(F32), source_yz.astype(F32)]
    pulse = jnp.concatenate([wavelet[0]] + place).reshape(1, 4)

    own_out, own_in, now_out, now_in = call(
        early_kernel,
        [stack(3 * REACH)] * 2 + [stack(REACH)] * 2,
        [H] * 3,
        [pltpu.SemaphoreType.DMA((6 * REACH,))],
        SMALL,
        SMALL,
    )(courant, now, adjoint)
    halo_out = lax.ppermute(own_out, "space", out_pairs)
    halo_in = lax.ppermute(own_in, "space", in_pairs)

    bands = jax.ShapeDtypeStruct((6, size_z, size_z), BF16)

    def half(outward, *given):
        return call(
            functools.partial(half_kernel, outward),
            [stack(REACH)] * 2 + [stack(2 * REACH)] + [bands] * outward,
            [V] * 3 + [H] * 2 + [V] * (not outward),
            [held(REACH)] * 2 + [pltpu.SemaphoreType.DMA((2 * REACH,))],
            LARGE,
            SMALL,
        )(*given)

    accel_out, adjoint_out, late_out, bands = half(True, own_out, own_in, now_out, old, late)
    if relayed:
        first_hop = lax.ppermute(late_out, "space", [(3, 7), (4, 0)])
        halo_lates = [
            lax.ppermute(late_out, "space", both_ways([(1, 2), (5, 6)])),
            lax.ppermute(first_hop, "space", [(7, 4), (0, 3)]),
        ]
    else:
        halo_lates = [lax.ppermute(late_out, "space", out_pairs)]
    accel_in, adjoint_in, late_in = half(False, own_in, own_out, now_in, old, late, bands)
    halo_late_in = lax.ppermute(late_in, "space", in_pairs)

    inner, outer_part, forward, backward, points_out = call(
        inner_kernel,
        [stack(2 * REACH), stack(3 * REACH)] + [stack(2 * REACH)] * 3,
        [V] * 17,
        [
            pltpu.VMEM((2 * slab * size_y, receiver_x.shape[1]), BF16),
            held(3 * slab),
            held(2 * REACH),
        ]
        + [held(REACH)] * 4,
        SMALL,
        SMALL,
    )(
        pulse,
        receiver_x,
        receiver_yz,
        residual_trace[0].T,
        own_in,
        own_out,
        accel_in,
        accel_out,
        adjoint_in,
        adjoint_out,
        late_in,
        late_out,
        now_in,
        now_out,
        bands,
        halo_in,
        halo_late_in,
    )
    outer, *inner_parts = call(
        functools.partial(middle_kernel, shots),
        [stack(4 * REACH)] + [(REACH, part_rows, size_z)] * shots,
        [V] * 8,
        [held(REACH)] * 3,
        LARGE,
        SMALL,
    )(own_in, own_out, bands, halo_out, inner, outer_part, forward, backward)
    shifts = [[(i, i ^ k) for i in range(shots)] for k in range(shots)]
    inner_parts = inner_parts[:1] + [
        lax.ppermute(inner_parts[k], "shot", shifts[k]) for k in range(1, shots)
    ]
    inner_sum = call(add_kernel, (REACH, part_rows, size_z), [V] * shots, [], LARGE, SMALL)(
        *inner_parts
    )
    outer_parts = call(
        functools.partial(outer_kernel, shots, relayed),
        [(REACH, part_rows, size_z)] * shots,
        [V] * (4 + len(halo_lates)),
        [held(2 * REACH)] + [held(REACH)] * 3,
        SMALL,
        SMALL,
    )(own_out, outer, halo_out, points_out, *halo_lates)
    outer_parts = list(outer_parts[:1]) + [
        lax.ppermute(outer_parts[k], "shot", shifts[k]) for k in range(1, shots)
    ]
    return call(sum_kernel, (slab, part_rows, size_z), [V] * (1 + shots), [], SMALL, SMALL)(
        inner_sum, *outer_parts
    )


def solution(mesh):
    field = P("shot", "space", None, None)
    specs = (
        P("space", None, None),
        field,
        field,
        field,
        field,
        P("shot"),
        P("shot"),
        P("shot", None),
        P("shot", None),
        P("shot", None),
        P("shot", None, None),
    )
    return jax.shard_map(
        on_device, mesh=mesh, in_specs=specs, out_specs=P("space", "shot", None), check_vma=False
    )
```

```python
import functools
import jax
import jax.numpy as jnp
from jax import lax
from jax.experimental import pallas as pl
from jax.experimental.pallas import tpu as pltpu
from jax.sharding import PartitionSpec as P

MIDDLE = 3.0 * (-205.0 / 72.0)
SIDE = (8.0 / 5.0, -1.0 / 5.0, 8.0 / 315.0, -1.0 / 560.0)
REACH = 4
EARLY_SPEEDS, INNER_SPEEDS = 3, 2
INWARD_ORDER, OUTWARD_ORDER = [2, 1, 3], [1, 2, 3]
F32 = jnp.float32
BF16 = jnp.bfloat16
VMEM_LIMIT = 32 * 1024 * 1024
MIDDLE_COST = int(6 * 10**9)
SECOND_COST = int(0.001 * 10**9)
SMALL, LARGE = 10**6, 10**10


def placed(layer, outward, odd):
    layer = layer if outward else 2 * REACH - 1 - layer
    return layer + odd * (2 * REACH - 1 - 2 * layer)


def grids(size_y, size_z):
    rows = lax.broadcasted_iota(jnp.int32, (size_y, size_z), 0)
    columns = lax.broadcasted_iota(jnp.int32, (size_y, size_z), 1)
    return rows, columns


def three_parts(values):
    high = values.astype(BF16)
    rest = values - high.astype(F32)
    middle = rest.astype(BF16)
    return high, middle, (rest - middle.astype(F32)).astype(BF16)


def exact_dot(left, right):
    def dot(a, b):
        return jnp.dot(left[a], right[b], preferred_element_type=F32)

    return dot(0, 0) + (dot(0, 1) + dot(1, 0)) + (dot(1, 1) + dot(0, 2) + dot(2, 0))


def band(size, block, middle):
    rows, columns = grids(size, size)
    distance = jnp.abs(rows - columns)
    weights = jnp.where(distance == 0, middle, 0.0)
    for offset in range(1, REACH + 1):
        weights = jnp.where(distance == offset, SIDE[offset - 1], weights)
    bits = block.bit_length() - 1
    return jnp.where(jnp.right_shift(rows, bits) == jnp.right_shift(columns, bits), weights, 0.0)


def plane_laplace(layers, along_y, along_z):
    shape = (len(layers),) + layers[0].shape
    parts = three_parts(jnp.concatenate(layers, axis=0))
    return (exact_dot(parts, along_z) + exact_dot(along_y, parts)).reshape(shape)


def weighted(terms):
    total = None
    for distance in range(1, REACH + 1):
        found = [layer() for at, layer in terms if at == distance]
        if found:
            term = SIDE[distance - 1] * functools.reduce(lambda a, b: a + b, found)
            total = term if total is None else total + term
    return total


def within(at, layers):
    return weighted([(abs(at - i), lambda i=i: layers(i)) for i in range(REACH) if i != at])


def from_other(at, layers):
    last = 2 * REACH - 1
    return weighted([(last - i - at, lambda i=i: layers(i)) for i in range(REACH)])


def across(at, layers):
    return weighted([(at + 1 + i, lambda i=i: layers(i)) for i in range(REACH)])


def add(*values):
    return functools.reduce(lambda a, b: a + b, [v for v in values if v is not None])


def early_kernel(courant, now, adjoint, packet, speeds, adjoints, sems):
    odd = lax.rem(lax.axis_index("space"), 2)
    copies = []
    for layer in range(REACH):
        at = placed(layer, True, odd)
        for source, target in ((courant, speeds), (adjoint, adjoints), (now, packet)):
            copies.append(
                pltpu.make_async_copy(source.at[at], target.at[layer], sems.at[len(copies)])
            )
            copies[-1].start()
    for copy in copies:
        copy.wait()
    for layer in range(REACH):
        speed = speeds[layer]
        packet[REACH + layer] = speed * speed * adjoints[layer]
        if layer < EARLY_SPEEDS:
            packet[2 * REACH + layer] = speed


def local_kernel(
    sent_first,
    courant,
    now,
    adjoint,
    old,
    late,
    accel,
    adjoint_mid,
    speeds,
    adjoint_now,
    bands,
    early_in,
    late_out,
    late_in,
    present,
    scaled,
    late_held,
    sem,
):
    size_y, size_z = courant.shape[1:]
    odd = lax.rem(lax.axis_index("space"), 2)
    copy = pltpu.make_async_copy(late, late_held, sem)
    copy.start()
    along_y = three_parts(band(REACH * size_y, size_y, 0.0))
    along_z = three_parts(band(size_z, size_z, MIDDLE))
    for number in range(3):
        bands[number] = along_y[number]
        bands[3 + number] = along_z[number]
    places = [placed(layer, half == 0, odd) for half in range(2) for layer in range(REACH)]
    for at, place in enumerate(places):
        speed = courant[place]
        speeds[at] = speed
        adjoint_now[at] = adjoint[place]
        present[at] = now[place]
        scaled[at] = speed * speed * adjoint[place]
    copy.wait()
    for half, packet in ((0, late_out), (1, late_in)):
        mine, other = half * REACH, (1 - half) * REACH
        flat = [
            plane_laplace([layers[mine + at] for at in range(REACH)], along_y, along_z)
            for layers in (present, scaled)
        ]
        for at in range(REACH):
            place = places[mine + at]
            speed_sq = speeds[mine + at] * speeds[mine + at]
            laplace = add(
                flat[0][at],
                within(at, lambda i: present[mine + i]),
                from_other(at, lambda i: present[other + i]),
            )
            accel[mine + at] = laplace
            packet[at] = 2.0 * now[place] - old[place] + speed_sq * laplace
            laplace = add(
                flat[1][at],
                within(at, lambda i: scaled[mine + i]),
                from_other(at, lambda i: scaled[other + i]),
            )
            field = 2.0 * adjoint[place] - late_held[place] + laplace
            adjoint_mid[mine + at] = field
            packet[REACH + at] = speed_sq * field
    for layer in range(EARLY_SPEEDS, REACH):
        late_out[2 * REACH + layer - EARLY_SPEEDS] = speeds[layer]
    for layer in range(REACH):
        early_in[layer] = present[REACH + layer]
        early_in[REACH + layer] = scaled[REACH + layer]
        if layer < INNER_SPEEDS:
            early_in[2 * REACH + layer] = speeds[REACH + layer]
        else:
            late_in[2 * REACH + layer - INNER_SPEEDS] = speeds[REACH + layer]


def next_halo(at, speed, late, own, points):
    speed_sq = speed * speed
    mid = late[at] + speed_sq * (across(at, lambda i: own[i]) + points[at])
    scaled = late[REACH + at] + speed_sq * (
        across(at, lambda i: own[REACH + i]) + points[REACH + at]
    )
    return mid, scaled


def exchange_order(shots, inward):
    if shots == 4:
        return [0] + (INWARD_ORDER if inward else OUTWARD_ORDER)
    return list(range(shots))


def scatter_rows(gradient, outputs, shots, inward):
    rows = gradient.shape[1] // shots
    me = lax.axis_index("shot")
    for number, shift in enumerate(exchange_order(shots, inward)):
        first = pl.multiple_of(jnp.bitwise_xor(me, shift) * rows, rows)
        outputs[number][...] = gradient[:, pl.ds(first, rows), :]


def inner_kernel(
    pulse,
    receiver_x,
    receiver_yz,
    residual,
    own_in,
    speeds,
    accel,
    adjoint_mid,
    late_in,
    late_out,
    adjoint_now,
    bands,
    halo_early,
    halo_late,
    inner,
    outer,
    forward,
    backward,
    points_out,
    marks,
    added,
    points_in,
    mid,
    scaled,
    next_mid,
    next_scaled,
):
    slab = 2 * REACH
    space = lax.axis_index("space")
    odd = lax.rem(space, 2)
    size_y, size_z = own_in.shape[1:]
    along_y, along_z = bands[0:3], bands[3:6]
    z_bits = size_z.bit_length() - 1

    def counted(x):
        local = x - space * slab
        return REACH + local + odd * (slab - 1 - 2 * local)

    cells = receiver_yz[...]
    layer = counted(receiver_x[...])
    inside = (layer >= 0) & (layer < 2 * slab)
    wanted = jnp.where(inside, layer * size_y + jnp.right_shift(cells, z_bits), -1)
    count = wanted.shape[1]
    line = lax.broadcasted_iota(jnp.int32, (2 * slab * size_y, count), 0)
    marks[...] = jnp.where(line == wanted, 1.0, 0.0).astype(BF16)
    depth = lax.broadcasted_iota(jnp.int32, (size_z, count), 0)
    hit = depth == jnp.bitwise_and(cells, size_z - 1)

    def received(step, first, last):
        total = None
        for part in three_parts(residual[pl.ds(step, 1), :]):
            spread = jnp.where(hit, part.astype(F32), 0.0).astype(BF16)
            term = lax.dot_general(
                marks[first * size_y : last * size_y],
                spread,
                (((1,), (1,)), ((), ())),
                preferred_element_type=F32,
            )
            total = term if total is None else total + term
        return total.reshape(last - first, size_y, size_z)

    added[0 : 2 * slab] = received(0, 0, 2 * slab)
    added[2 * slab :] = received(1, REACH, REACH + slab)

    rows, columns = grids(size_y, size_z)
    cell = rows * size_z + columns
    source_layer = counted(pulse[:, 2:3].astype(jnp.int32))
    source_cell = pulse[:, 3:4].astype(jnp.int32)

    def fired(step, at):
        spot = jnp.where(source_layer == at, source_cell, -1)
        return jnp.where(cell == spot, pulse[:, step : step + 1], 0.0)

    for at in range(REACH):
        points_out[at] = fired(0, REACH - 1 - at)
        points_out[REACH + at] = added[REACH - 1 - at]
        points_in[at] = fired(0, REACH + slab + at)
        points_in[REACH + at] = added[REACH + slab + at]
        speed = speeds[at]
        fire = fired(0, REACH + at)
        outer[at] = accel[at] + fire
        outer[REACH + at] = adjoint_mid[at] + added[REACH + at]
        outer[2 * REACH + at] = late_out[at] + speed * speed * fire
    for at in range(REACH):
        if at < INNER_SPEEDS:
            speed = halo_early[2 * REACH + at]
        else:
            speed = halo_late[2 * REACH + at - INNER_SPEEDS]
        next_mid[at], next_scaled[at] = next_halo(at, speed, halo_late, own_in, points_in)
    for at in range(REACH):
        to = REACH + slab - 1 - at
        speed = speeds[REACH + at]
        speed_sq = speed * speed
        extra = across(at, lambda i: halo_early[i]) + fired(0, to)
        adjoint = adjoint_mid[REACH + at] + across(at, lambda i: halo_early[REACH + i]) + added[to]
        inner[at] = accel[REACH + at] + extra
        inner[REACH + at] = adjoint
        mid[at] = late_in[at] + speed_sq * extra
        scaled[at] = speed_sq * adjoint
    flat_mid = plane_laplace([mid[at] for at in range(REACH)], along_y, along_z)
    flat_scaled = plane_laplace([scaled[at] for at in range(REACH)], along_y, along_z)
    for at in range(REACH):
        to = REACH + at
        forward[at] = add(fired(1, to), from_other(at, lambda i: mid[i]))
        backward[at] = add(
            added[2 * slab + at] - adjoint_now[at],
            from_other(at, lambda i: scaled[i]),
        )
        to = REACH + slab - 1 - at
        forward[REACH + at] = add(
            flat_mid[at],
            fired(1, to),
            within(at, lambda i: mid[i]),
            across(at, lambda i: next_mid[i]),
        )
        backward[REACH + at] = add(
            flat_scaled[at],
            added[2 * slab + slab - 1 - at] - adjoint_now[REACH + at],
            2.0 * inner[REACH + at],
            within(at, lambda i: scaled[i]),
            across(at, lambda i: next_scaled[i]),
        )


def middle_kernel(shots, speeds, halo, inner, outer_part, forward, backward, outer, step, *rest):
    outputs, (gradient,) = rest[:shots], rest[shots:]
    for at in range(REACH):
        speed = speeds[at]
        speed_sq = speed * speed
        extra = across(at, lambda i: halo[i])
        adjoint = outer_part[REACH + at] + across(at, lambda i: halo[REACH + i])
        outer[at] = outer_part[at] + extra
        outer[REACH + at] = adjoint
        step[at] = outer_part[2 * REACH + at] + speed_sq * extra
        step[REACH + at] = speed_sq * adjoint
    for at in range(REACH):
        ahead = add(forward[REACH + at], from_other(at, lambda i: step[i]))
        back = add(backward[REACH + at], from_other(at, lambda i: step[REACH + i]))
        speed = speeds[REACH + at]
        gradient[at] = 2.0 * speed * (back * inner[at] + inner[REACH + at] * ahead)
    scatter_rows(gradient, outputs, shots, True)


def second_kernel(bands, outer, step, forward, backward, after):
    along_y, along_z = bands[0:3], bands[3:6]
    flat_mid = plane_laplace([step[at] for at in range(REACH)], along_y, along_z)
    flat_scaled = plane_laplace([step[REACH + at] for at in range(REACH)], along_y, along_z)
    for at in range(REACH):
        after[at] = add(forward[at], flat_mid[at], within(at, lambda i: step[i]))
        after[REACH + at] = add(
            backward[at],
            2.0 * outer[REACH + at],
            flat_scaled[at],
            within(at, lambda i: step[REACH + i]),
        )


def outer_kernel(shots, relayed, own_out, speeds, outer, after, halo_early, points_out, *rest):
    lates, rest = rest[: 1 + relayed], rest[1 + relayed :]
    outputs, (late, next_mid, next_scaled, gradient) = rest[:shots], rest[shots:]
    if relayed:
        for layer in range(late.shape[0]):
            late[layer] = lates[0][layer] + lates[1][layer]
    else:
        late = lates[0]
    for at in range(REACH):
        if at < EARLY_SPEEDS:
            speed = halo_early[2 * REACH + at]
        else:
            speed = late[2 * REACH + at - EARLY_SPEEDS]
        next_mid[at], next_scaled[at] = next_halo(at, speed, late, own_out, points_out)
    for at in range(REACH):
        ahead = after[at] + across(at, lambda i: next_mid[i])
        back = after[REACH + at] + across(at, lambda i: next_scaled[i])
        speed = speeds[at]
        gradient[at] = 2.0 * speed * (back * outer[at] + outer[REACH + at] * ahead)
    scatter_rows(gradient, outputs, shots, False)


def add_kernel(*refs):
    refs[-1][...] = functools.reduce(lambda a, b: a + b, [ref[...] for ref in refs[:-1]])


def sum_kernel(inner, *refs):
    outers, out = refs[:-1], refs[-1]
    odd = lax.rem(lax.axis_index("space"), 2)
    for at in range(REACH):
        out[placed(at, True, odd)] = functools.reduce(lambda a, b: a + b, [r[at] for r in outers])
        out[placed(at, False, odd)] = inner[at]


def call(kernel, shapes, in_spaces, scratch, flops, moved):
    def shape(given):
        return jax.ShapeDtypeStruct(given, F32) if isinstance(given, tuple) else given

    many = isinstance(shapes, list)
    return pl.pallas_call(
        kernel,
        out_shape=[shape(s) for s in shapes] if many else shape(shapes),
        in_specs=[pl.BlockSpec(memory_space=space) for space in in_spaces],
        out_specs=[pl.BlockSpec(memory_space=pltpu.VMEM) for _ in shapes]
        if many
        else pl.BlockSpec(memory_space=pltpu.VMEM),
        scratch_shapes=scratch,
        compiler_params=pltpu.CompilerParams(vmem_limit_bytes=VMEM_LIMIT),
        cost_estimate=pl.CostEstimate(flops=flops, bytes_accessed=moved, transcendentals=0),
    )


def both_ways(pairs):
    return pairs + [(b, a) for a, b in pairs]


def on_device(
    courant,
    field_old,
    field_now,
    adjoint_late,
    adjoint_now,
    source_x,
    source_yz,
    wavelet,
    receiver_x,
    receiver_yz,
    residual_trace,
):
    slab, size_y, size_z = courant.shape
    if slab != 2 * REACH:
        raise ValueError("unsupported slab")
    shots = lax.axis_size("shot")
    devices = lax.axis_size("space")
    plane = size_y * size_z
    part_rows = size_y // shots
    V, H = pltpu.VMEM, pltpu.HBM

    def stack(layers):
        return (layers, size_y, size_z)

    def held(layers):
        return pltpu.VMEM(stack(layers), F32)

    def in_hbm(values):
        return pltpu.with_memory_space_constraint(values, pltpu.HBM)

    out_pairs = both_ways([(i, i + 1) for i in range(1, devices - 1, 2)])
    in_pairs = [(i, i ^ 1) for i in range(devices)]
    relayed = devices == 8
    old, now, late, adjoint = (
        field[0] for field in (field_old, field_now, adjoint_late, adjoint_now)
    )
    place = [source_x.astype(F32), source_yz.astype(F32)]
    pulse = jnp.concatenate([wavelet[0]] + place).reshape(1, 4)

    early_layers = 2 * REACH + EARLY_SPEEDS
    late_layers = 3 * REACH - EARLY_SPEEDS
    early_out = call(
        early_kernel,
        stack(early_layers),
        [H] * 3,
        [held(REACH)] * 2 + [pltpu.SemaphoreType.DMA((3 * REACH,))],
        SMALL,
        SMALL,
    )(in_hbm(courant), in_hbm(now), in_hbm(adjoint))
    halo_out = lax.ppermute(early_out, "space", out_pairs)

    bands = jax.ShapeDtypeStruct((6, size_z, size_z), BF16)
    accel, adjoint_mid, speeds, adjoint_half, bands, early_in, late_out, late_in = call(
        local_kernel,
        [stack(slab)] * 4
        + [bands, stack(2 * REACH + INNER_SPEEDS), stack(late_layers)]
        + [stack(3 * REACH - INNER_SPEEDS)],
        [pl.ANY] + [V] * 4 + [H],
        [held(slab)] * 3 + [pltpu.SemaphoreType.DMA(())],
        LARGE,
        SMALL,
    )(early_out, courant, now, adjoint, old, in_hbm(late))
    halo_in = lax.ppermute(early_in, "space", in_pairs)
    halo_late_in = lax.ppermute(late_in, "space", in_pairs)
    if relayed:
        first_hop = lax.ppermute(late_out, "space", [(3, 7), (4, 0)])
        halo_lates = [lax.ppermute(late_out, "space", both_ways([(1, 2), (5, 6)]))]
    else:
        halo_lates = [lax.ppermute(late_out, "space", out_pairs)]
    inner, outer_part, forward, backward, points_out = call(
        inner_kernel,
        [stack(2 * REACH), stack(3 * REACH)] + [stack(2 * REACH)] * 3,
        [V] * 14,
        [
            pltpu.VMEM((2 * slab * size_y, receiver_x.shape[1]), BF16),
            held(3 * slab),
            held(2 * REACH),
        ]
        + [held(REACH)] * 4,
        SMALL,
        SMALL,
    )(
        pulse,
        receiver_x,
        receiver_yz,
        residual_trace[0].T,
        early_in,
        speeds,
        accel,
        adjoint_mid,
        late_in,
        late_out,
        adjoint_half,
        bands,
        halo_in,
        halo_late_in,
    )
    if relayed:
        first_hop, inner = lax.optimization_barrier((first_hop, inner))
        halo_lates.append(lax.ppermute(first_hop, "space", [(7, 4), (0, 3)]))
    outer, step, *inner_parts = call(
        functools.partial(middle_kernel, shots),
        [stack(2 * REACH)] * 2 + [(REACH, part_rows, size_z)] * shots,
        [V] * 6,
        [held(REACH)],
        MIDDLE_COST,
        SMALL,
    )(speeds, halo_out, inner, outer_part, forward, backward)
    after = call(second_kernel, stack(2 * REACH), [V] * 5, [], SECOND_COST, SMALL)(
        bands, outer, step, forward, backward
    )
    shifts = [
        [[(i, i ^ k) for i in range(shots)] for k in exchange_order(shots, inward)]
        for inward in (True, False)
    ]
    inner_parts = inner_parts[:1] + [
        lax.ppermute(inner_parts[k], "shot", shifts[0][k]) for k in range(1, shots)
    ]
    inner_sum = call(add_kernel, (REACH, part_rows, size_z), [V] * shots, [], LARGE, SMALL)(
        *inner_parts
    )
    outer_parts = call(
        functools.partial(outer_kernel, shots, relayed),
        [(REACH, part_rows, size_z)] * shots,
        [V] * (6 + len(halo_lates)),
        [held(late_layers)] + [held(REACH)] * 3,
        SMALL,
        SMALL,
    )(early_out, speeds, outer, after, halo_out, points_out, *halo_lates)
    outer_parts = list(outer_parts[:1]) + [
        lax.ppermute(outer_parts[k], "shot", shifts[1][k]) for k in range(1, shots)
    ]
    return call(sum_kernel, (slab, part_rows, size_z), [V] * (1 + shots), [], SMALL, SMALL)(
        inner_sum, *outer_parts
    )


def solution(mesh):
    field = P("shot", "space", None, None)
    specs = (
        P("space", None, None),
        field,
        field,
        field,
        field,
        P("shot"),
        P("shot"),
        P("shot", None),
        P("shot", None),
        P("shot", None),
        P("shot", None, None),
    )
    return jax.shard_map(
        on_device, mesh=mesh, in_specs=specs, out_specs=P("space", "shot", None), check_vma=False
    )
```

```python
import functools
import jax
import jax.numpy as jnp
from jax import lax
from jax.experimental import pallas as pl
from jax.experimental.pallas import tpu as pltpu
from jax.sharding import PartitionSpec as P

MIDDLE = 3.0 * (-205.0 / 72.0)
SIDE = (8.0 / 5.0, -1.0 / 5.0, 8.0 / 315.0, -1.0 / 560.0)
REACH = 4
SCALE = 5040.0
WHOLE_SIDE = (8064.0, -1008.0, 128.0, -9.0)
EARLY_SPEEDS, INNER_SPEEDS = 3, 2
INWARD_ORDER, OUTWARD_ORDER = [2, 1, 3], [1, 2, 3]
F32 = jnp.float32
BF16 = jnp.bfloat16
VMEM_LIMIT = 32 * 1024 * 1024
MIDDLE_COST = int(6 * 10**9)
SECOND_COST = int(0.001 * 10**9)
SMALL, LARGE = 10**6, 10**10


def placed(layer, outward, odd):
    layer = layer if outward else 2 * REACH - 1 - layer
    return layer + odd * (2 * REACH - 1 - 2 * layer)


def grids(size_y, size_z):
    rows = lax.broadcasted_iota(jnp.int32, (size_y, size_z), 0)
    columns = lax.broadcasted_iota(jnp.int32, (size_y, size_z), 1)
    return rows, columns


def three_parts(values):
    high = values.astype(BF16)
    rest = values - high.astype(F32)
    middle = rest.astype(BF16)
    return high, middle, (rest - middle.astype(F32)).astype(BF16)


def band(size, block):
    rows, columns = grids(size, size)
    distance = jnp.abs(rows - columns)
    weights = jnp.zeros((size, size), F32)
    for offset in range(1, REACH + 1):
        weights = jnp.where(distance == offset, WHOLE_SIDE[offset - 1], weights)
    bits = block.bit_length() - 1
    same = jnp.right_shift(rows, bits) == jnp.right_shift(columns, bits)
    return jnp.where(same, weights, 0.0).astype(BF16)


def plane_laplace(layers, along_y, along_z):
    shape = (len(layers),) + layers[0].shape
    values = jnp.concatenate(layers, axis=0)
    total = None
    for part in three_parts(values)[::-1]:
        term = jnp.dot(part, along_z, preferred_element_type=F32)
        term += jnp.dot(along_y, part, preferred_element_type=F32)
        total = term if total is None else total + term
    return (total * (1.0 / SCALE) + MIDDLE * values).reshape(shape)


def weighted(terms):
    total = None
    for distance in range(1, REACH + 1):
        found = [layer() for at, layer in terms if at == distance]
        if found:
            term = SIDE[distance - 1] * functools.reduce(lambda a, b: a + b, found)
            total = term if total is None else total + term
    return total


def within(at, layers):
    return weighted([(abs(at - i), lambda i=i: layers(i)) for i in range(REACH) if i != at])


def from_other(at, layers):
    last = 2 * REACH - 1
    return weighted([(last - i - at, lambda i=i: layers(i)) for i in range(REACH)])


def across(at, layers):
    return weighted([(at + 1 + i, lambda i=i: layers(i)) for i in range(REACH)])


def add(*values):
    return functools.reduce(lambda a, b: a + b, [v for v in values if v is not None])


def early_kernel(courant, now, adjoint, packet, speeds, fields, adjoints, sems):
    odd = lax.rem(lax.axis_index("space"), 2)
    pairs = ((courant, speeds), (adjoint, adjoints), (now, fields))
    copies = [
        pltpu.make_async_copy(source.at[pl.ds(odd * REACH, REACH)], target, sems.at[number])
        for number, (source, target) in enumerate(pairs)
    ]
    for copy in copies:
        copy.start()
    for copy in copies:
        copy.wait()
    for layer in range(REACH):
        at = layer + odd * (REACH - 1 - 2 * layer)
        speed = speeds[at]
        packet[layer] = fields[at]
        packet[REACH + layer] = speed * speed * adjoints[at]
        if layer < EARLY_SPEEDS:
            packet[2 * REACH + layer] = speed


def local_kernel(
    sent_first,
    courant,
    now,
    adjoint,
    old,
    late,
    accel,
    adjoint_mid,
    speeds,
    adjoint_now,
    bands,
    early_in,
    late_out,
    late_in,
    present,
    scaled,
    late_held,
    sem,
):
    size_y, size_z = courant.shape[1:]
    odd = lax.rem(lax.axis_index("space"), 2)
    copy = pltpu.make_async_copy(late, late_held, sem)
    copy.start()
    along_y, along_z = band(REACH * size_y, size_y), band(size_z, size_z)
    bands[0] = along_y
    bands[1] = along_z
    places = [placed(layer, half == 0, odd) for half in range(2) for layer in range(REACH)]
    for at, place in enumerate(places):
        speed = courant[place]
        speeds[at] = speed
        adjoint_now[at] = adjoint[place]
        present[at] = now[place]
        scaled[at] = speed * speed * adjoint[place]
    for mine, packet in ((0, late_out), (REACH, late_in)):
        other = REACH - mine
        flat = [
            plane_laplace([layers[mine + at] for at in range(REACH)], along_y, along_z)
            for layers in (present, scaled)
        ]
        if mine == 0:
            copy.wait()
        for at in range(REACH):
            place = places[mine + at]
            speed_sq = speeds[mine + at] * speeds[mine + at]
            laplace = add(
                flat[0][at],
                within(at, lambda i: present[mine + i]),
                from_other(at, lambda i: present[other + i]),
            )
            accel[mine + at] = laplace
            packet[at] = 2.0 * now[place] - old[place] + speed_sq * laplace
            laplace = add(
                flat[1][at],
                within(at, lambda i: scaled[mine + i]),
                from_other(at, lambda i: scaled[other + i]),
            )
            field = 2.0 * adjoint[place] - late_held[place] + laplace
            adjoint_mid[mine + at] = field
            packet[REACH + at] = speed_sq * field
    for layer in range(EARLY_SPEEDS, REACH):
        late_out[2 * REACH + layer - EARLY_SPEEDS] = speeds[layer]
    for layer in range(REACH):
        early_in[layer] = present[REACH + layer]
        early_in[REACH + layer] = scaled[REACH + layer]
        if layer < INNER_SPEEDS:
            early_in[2 * REACH + layer] = speeds[REACH + layer]
        else:
            late_in[2 * REACH + layer - INNER_SPEEDS] = speeds[REACH + layer]


def next_halo(at, speed, late, own, points):
    speed_sq = speed * speed
    mid = late[at] + speed_sq * (across(at, lambda i: own[i]) + points[at])
    scaled = late[REACH + at] + speed_sq * (
        across(at, lambda i: own[REACH + i]) + points[REACH + at]
    )
    return mid, scaled


def exchange_order(shots, inward):
    if shots == 4:
        return [0] + (INWARD_ORDER if inward else OUTWARD_ORDER)
    return list(range(shots))


def scatter_rows(gradient, outputs, shots, inward):
    rows = gradient.shape[1] // shots
    me = lax.axis_index("shot")
    for number, shift in enumerate(exchange_order(shots, inward)):
        first = pl.multiple_of(jnp.bitwise_xor(me, shift) * rows, rows)
        outputs[number][...] = gradient[:, pl.ds(first, rows), :]


def inner_kernel(
    pulse,
    receiver_x,
    receiver_yz,
    residual,
    own_in,
    speeds,
    accel,
    adjoint_mid,
    late_in,
    late_out,
    adjoint_now,
    bands,
    halo_early,
    halo_late,
    inner,
    outer,
    forward,
    backward,
    points_out,
    marks,
    added,
    points_in,
    mid,
    scaled,
    next_mid,
    next_scaled,
):
    slab = 2 * REACH
    space = lax.axis_index("space")
    odd = lax.rem(space, 2)
    size_y, size_z = own_in.shape[1:]
    along_y, along_z = bands[0], bands[1]
    z_bits = size_z.bit_length() - 1

    def counted(x):
        local = x - space * slab
        return REACH + local + odd * (slab - 1 - 2 * local)

    cells = receiver_yz[...]
    layer = counted(receiver_x[...])
    inside = (layer >= 0) & (layer < 2 * slab)
    wanted = jnp.where(inside, layer * size_y + jnp.right_shift(cells, z_bits), -1)
    count = wanted.shape[1]
    line = lax.broadcasted_iota(jnp.int32, (2 * slab * size_y, count), 0)
    marks[...] = jnp.where(line == wanted, 1.0, 0.0).astype(BF16)
    depth = lax.broadcasted_iota(jnp.int32, (size_z, count), 0)
    hit = depth == jnp.bitwise_and(cells, size_z - 1)

    def received(step, first, last):
        total = None
        for part in three_parts(residual[pl.ds(step, 1), :]):
            spread = jnp.where(hit, part.astype(F32), 0.0).astype(BF16)
            term = lax.dot_general(
                marks[first * size_y : last * size_y],
                spread,
                (((1,), (1,)), ((), ())),
                preferred_element_type=F32,
            )
            total = term if total is None else total + term
        return total.reshape(last - first, size_y, size_z)

    added[0 : 2 * slab] = received(0, 0, 2 * slab)
    added[2 * slab :] = received(1, REACH, REACH + slab)

    rows, columns = grids(size_y, size_z)
    cell = rows * size_z + columns
    source_layer = counted(pulse[:, 2:3].astype(jnp.int32))
    source_cell = pulse[:, 3:4].astype(jnp.int32)

    def fired(step, at):
        spot = jnp.where(source_layer == at, source_cell, -1)
        return jnp.where(cell == spot, pulse[:, step : step + 1], 0.0)

    for at in range(REACH):
        points_out[at] = fired(0, REACH - 1 - at)
        points_out[REACH + at] = added[REACH - 1 - at]
        points_in[at] = fired(0, REACH + slab + at)
        points_in[REACH + at] = added[REACH + slab + at]
        speed = speeds[at]
        fire = fired(0, REACH + at)
        outer[at] = accel[at] + fire
        outer[REACH + at] = adjoint_mid[at] + added[REACH + at]
        outer[2 * REACH + at] = late_out[at] + speed * speed * fire
    for at in range(REACH):
        if at < INNER_SPEEDS:
            speed = halo_early[2 * REACH + at]
        else:
            speed = halo_late[2 * REACH + at - INNER_SPEEDS]
        next_mid[at], next_scaled[at] = next_halo(at, speed, halo_late, own_in, points_in)
    for at in range(REACH):
        to = REACH + slab - 1 - at
        speed = speeds[REACH + at]
        speed_sq = speed * speed
        extra = across(at, lambda i: halo_early[i]) + fired(0, to)
        adjoint = adjoint_mid[REACH + at] + across(at, lambda i: halo_early[REACH + i]) + added[to]
        inner[at] = accel[REACH + at] + extra
        inner[REACH + at] = adjoint
        mid[at] = late_in[at] + speed_sq * extra
        scaled[at] = speed_sq * adjoint
    flat_mid = plane_laplace([mid[at] for at in range(REACH)], along_y, along_z)
    flat_scaled = plane_laplace([scaled[at] for at in range(REACH)], along_y, along_z)
    for at in range(REACH):
        to = REACH + at
        forward[at] = add(fired(1, to), from_other(at, lambda i: mid[i]))
        backward[at] = add(
            added[2 * slab + at] - adjoint_now[at],
            from_other(at, lambda i: scaled[i]),
        )
        to = REACH + slab - 1 - at
        forward[REACH + at] = add(
            flat_mid[at],
            fired(1, to),
            within(at, lambda i: mid[i]),
            across(at, lambda i: next_mid[i]),
        )
        backward[REACH + at] = add(
            flat_scaled[at],
            added[2 * slab + slab - 1 - at] - adjoint_now[REACH + at],
            2.0 * inner[REACH + at],
            within(at, lambda i: scaled[i]),
            across(at, lambda i: next_scaled[i]),
        )


def middle_kernel(shots, speeds, halo, inner, outer_part, forward, backward, outer, step, *rest):
    outputs, (gradient,) = rest[:shots], rest[shots:]
    for at in range(REACH):
        speed = speeds[at]
        speed_sq = speed * speed
        extra = across(at, lambda i: halo[i])
        adjoint = outer_part[REACH + at] + across(at, lambda i: halo[REACH + i])
        outer[at] = outer_part[at] + extra
        outer[REACH + at] = adjoint
        step[at] = outer_part[2 * REACH + at] + speed_sq * extra
        step[REACH + at] = speed_sq * adjoint
    for at in range(REACH):
        ahead = add(forward[REACH + at], from_other(at, lambda i: step[i]))
        back = add(backward[REACH + at], from_other(at, lambda i: step[REACH + i]))
        speed = speeds[REACH + at]
        gradient[at] = 2.0 * speed * (back * inner[at] + inner[REACH + at] * ahead)
    scatter_rows(gradient, outputs, shots, True)


def second_kernel(bands, outer, step, forward, backward, after):
    along_y, along_z = bands[0], bands[1]
    flat_mid = plane_laplace([step[at] for at in range(REACH)], along_y, along_z)
    flat_scaled = plane_laplace([step[REACH + at] for at in range(REACH)], along_y, along_z)
    for at in range(REACH):
        after[at] = add(forward[at], flat_mid[at], within(at, lambda i: step[i]))
        after[REACH + at] = add(
            backward[at],
            2.0 * outer[REACH + at],
            flat_scaled[at],
            within(at, lambda i: step[REACH + i]),
        )


def outer_kernel(shots, relayed, own_out, speeds, outer, after, halo_early, points_out, *rest):
    lates, rest = rest[: 1 + relayed], rest[1 + relayed :]
    outputs, (late, next_mid, next_scaled, gradient) = rest[:shots], rest[shots:]
    if relayed:
        for layer in range(late.shape[0]):
            late[layer] = lates[0][layer] + lates[1][layer]
    else:
        late = lates[0]
    for at in range(REACH):
        if at < EARLY_SPEEDS:
            speed = halo_early[2 * REACH + at]
        else:
            speed = late[2 * REACH + at - EARLY_SPEEDS]
        next_mid[at], next_scaled[at] = next_halo(at, speed, late, own_out, points_out)
    for at in range(REACH):
        ahead = after[at] + across(at, lambda i: next_mid[i])
        back = after[REACH + at] + across(at, lambda i: next_scaled[i])
        speed = speeds[at]
        gradient[at] = 2.0 * speed * (back * outer[at] + outer[REACH + at] * ahead)
    scatter_rows(gradient, outputs, shots, False)


def add_kernel(*refs):
    refs[-1][...] = functools.reduce(lambda a, b: a + b, [ref[...] for ref in refs[:-1]])


def sum_kernel(inner, *refs):
    outers, out = refs[:-1], refs[-1]
    odd = lax.rem(lax.axis_index("space"), 2)
    for at in range(REACH):
        out[placed(at, True, odd)] = functools.reduce(lambda a, b: a + b, [r[at] for r in outers])
        out[placed(at, False, odd)] = inner[at]


def call(kernel, shapes, in_spaces, scratch, flops, moved):
    def shape(given):
        return jax.ShapeDtypeStruct(given, F32) if isinstance(given, tuple) else given

    many = isinstance(shapes, list)
    return pl.pallas_call(
        kernel,
        out_shape=[shape(s) for s in shapes] if many else shape(shapes),
        in_specs=[pl.BlockSpec(memory_space=space) for space in in_spaces],
        out_specs=[pl.BlockSpec(memory_space=pltpu.VMEM) for _ in shapes]
        if many
        else pl.BlockSpec(memory_space=pltpu.VMEM),
        scratch_shapes=scratch,
        compiler_params=pltpu.CompilerParams(vmem_limit_bytes=VMEM_LIMIT),
        cost_estimate=pl.CostEstimate(flops=flops, bytes_accessed=moved, transcendentals=0),
    )


def both_ways(pairs):
    return pairs + [(b, a) for a, b in pairs]


def on_device(
    courant,
    field_old,
    field_now,
    adjoint_late,
    adjoint_now,
    source_x,
    source_yz,
    wavelet,
    receiver_x,
    receiver_yz,
    residual_trace,
):
    slab, size_y, size_z = courant.shape
    if slab != 2 * REACH:
        raise ValueError("unsupported slab")
    shots = lax.axis_size("shot")
    devices = lax.axis_size("space")
    plane = size_y * size_z
    part_rows = size_y // shots
    V, H = pltpu.VMEM, pltpu.HBM

    def stack(layers):
        return (layers, size_y, size_z)

    def held(layers):
        return pltpu.VMEM(stack(layers), F32)

    def in_hbm(values):
        return pltpu.with_memory_space_constraint(values, pltpu.HBM)

    out_pairs = both_ways([(i, i + 1) for i in range(1, devices - 1, 2)])
    in_pairs = [(i, i ^ 1) for i in range(devices)]
    relayed = devices == 8
    old, now, late, adjoint = (
        field[0] for field in (field_old, field_now, adjoint_late, adjoint_now)
    )
    place = [source_x.astype(F32), source_yz.astype(F32)]
    pulse = jnp.concatenate([wavelet[0]] + place).reshape(1, 4)

    early_layers = 2 * REACH + EARLY_SPEEDS
    late_layers = 3 * REACH - EARLY_SPEEDS
    early_out = call(
        early_kernel,
        stack(early_layers),
        [H] * 3,
        [held(REACH)] * 3 + [pltpu.SemaphoreType.DMA((3,))],
        SMALL,
        SMALL,
    )(in_hbm(courant), in_hbm(now), in_hbm(adjoint))
    halo_out = lax.ppermute(early_out, "space", out_pairs)

    bands = jax.ShapeDtypeStruct((2, size_z, size_z), BF16)
    accel, adjoint_mid, speeds, adjoint_half, bands, early_in, late_out, late_in = call(
        local_kernel,
        [stack(slab)] * 4
        + [bands, stack(2 * REACH + INNER_SPEEDS), stack(late_layers)]
        + [stack(3 * REACH - INNER_SPEEDS)],
        [pl.ANY] + [V] * 4 + [H],
        [held(slab)] * 3 + [pltpu.SemaphoreType.DMA(())],
        LARGE,
        SMALL,
    )(early_out, courant, now, adjoint, old, in_hbm(late))
    halo_in = lax.ppermute(early_in, "space", in_pairs)
    halo_late_in = lax.ppermute(late_in, "space", in_pairs)
    if relayed:
        first_hop = lax.ppermute(late_out, "space", [(3, 7), (4, 0)])
        halo_lates = [lax.ppermute(late_out, "space", both_ways([(1, 2), (5, 6)]))]
    else:
        halo_lates = [lax.ppermute(late_out, "space", out_pairs)]
    inner, outer_part, forward, backward, points_out = call(
        inner_kernel,
        [stack(2 * REACH), stack(3 * REACH)] + [stack(2 * REACH)] * 3,
        [V] * 14,
        [
            pltpu.VMEM((2 * slab * size_y, receiver_x.shape[1]), BF16),
            held(3 * slab),
            held(2 * REACH),
        ]
        + [held(REACH)] * 4,
        SMALL,
        SMALL,
    )(
        pulse,
        receiver_x,
        receiver_yz,
        residual_trace[0].T,
        early_in,
        speeds,
        accel,
        adjoint_mid,
        late_in,
        late_out,
        adjoint_half,
        bands,
        halo_in,
        halo_late_in,
    )
    if relayed:
        first_hop, inner = lax.optimization_barrier((first_hop, inner))
        halo_lates.append(lax.ppermute(first_hop, "space", [(7, 4), (0, 3)]))
    outer, step, *inner_parts = call(
        functools.partial(middle_kernel, shots),
        [stack(2 * REACH)] * 2 + [(REACH, part_rows, size_z)] * shots,
        [V] * 6,
        [held(REACH)],
        MIDDLE_COST,
        SMALL,
    )(speeds, halo_out, inner, outer_part, forward, backward)
    after = call(second_kernel, stack(2 * REACH), [V] * 5, [], SECOND_COST, SMALL)(
        bands, outer, step, forward, backward
    )
    shifts = [
        [[(i, i ^ k) for i in range(shots)] for k in exchange_order(shots, inward)]
        for inward in (True, False)
    ]
    inner_parts = inner_parts[:1] + [
        lax.ppermute(inner_parts[k], "shot", shifts[0][k]) for k in range(1, shots)
    ]
    inner_sum = call(add_kernel, (REACH, part_rows, size_z), [V] * shots, [], LARGE, SMALL)(
        *inner_parts
    )
    outer_parts = call(
        functools.partial(outer_kernel, shots, relayed),
        [(REACH, part_rows, size_z)] * shots,
        [V] * (6 + len(halo_lates)),
        [held(late_layers)] + [held(REACH)] * 3,
        SMALL,
        SMALL,
    )(early_out, speeds, outer, after, halo_out, points_out, *halo_lates)
    outer_parts = list(outer_parts[:1]) + [
        lax.ppermute(outer_parts[k], "shot", shifts[1][k]) for k in range(1, shots)
    ]
    return call(sum_kernel, (slab, part_rows, size_z), [V] * (1 + shots), [], SMALL, SMALL)(
        inner_sum, *outer_parts
    )


def solution(mesh):
    field = P("shot", "space", None, None)
    specs = (
        P("space", None, None),
        field,
        field,
        field,
        field,
        P("shot"),
        P("shot"),
        P("shot", None),
        P("shot", None),
        P("shot", None),
        P("shot", None, None),
    )
    return jax.shard_map(
        on_device, mesh=mesh, in_specs=specs, out_specs=P("space", "shot", None), check_vma=False
    )
```

```python
import functools
import jax
import jax.numpy as jnp
from jax import lax
from jax.experimental import pallas as pl
from jax.experimental.pallas import tpu as pltpu
from jax.sharding import PartitionSpec as P

MIDDLE = 3.0 * (-205.0 / 72.0)
SIDE = (8.0 / 5.0, -1.0 / 5.0, 8.0 / 315.0, -1.0 / 560.0)
REACH = 4
SCALE = 5040.0
WHOLE_SIDE = (8064.0, -1008.0, 128.0, -9.0)
EARLY_SPEEDS, INNER_SPEEDS = 2, 2
EARLY_EXTRA, LATE_EXTRA = 16, 8
INWARD_ORDER, OUTWARD_ORDER = [2, 3, 1], [1, 2, 3]
F32 = jnp.float32
BF16 = jnp.bfloat16
VMEM_LIMIT = 32 * 1024 * 1024
MIDDLE_COST = int(8 * 10**9)
SECOND_COST = int(0.001 * 10**9)
SMALL, LARGE = 10**6, 10**10


def placed(layer, outward, odd):
    layer = layer if outward else 2 * REACH - 1 - layer
    return layer + odd * (2 * REACH - 1 - 2 * layer)


def grids(size_y, size_z):
    rows = lax.broadcasted_iota(jnp.int32, (size_y, size_z), 0)
    columns = lax.broadcasted_iota(jnp.int32, (size_y, size_z), 1)
    return rows, columns


def three_parts(values):
    high = values.astype(BF16)
    rest = values - high.astype(F32)
    middle = rest.astype(BF16)
    return high, middle, (rest - middle.astype(F32)).astype(BF16)


def band(size, block):
    rows, columns = grids(size, size)
    distance = jnp.abs(rows - columns)
    weights = jnp.zeros((size, size), F32)
    for offset in range(1, REACH + 1):
        weights = jnp.where(distance == offset, WHOLE_SIDE[offset - 1], weights)
    bits = block.bit_length() - 1
    same = jnp.right_shift(rows, bits) == jnp.right_shift(columns, bits)
    return jnp.where(same, weights, 0.0).astype(BF16)


def plane_laplace(layers, along_y, along_z):
    shape = (len(layers),) + layers[0].shape
    values = jnp.concatenate(layers, axis=0)
    total = None
    for part in three_parts(values)[::-1]:
        term = jnp.dot(part, along_z, preferred_element_type=F32)
        term += jnp.dot(along_y, part, preferred_element_type=F32)
        total = term if total is None else total + term
    return (total * (1.0 / SCALE) + MIDDLE * values).reshape(shape)


def weighted(terms):
    total = None
    for distance in range(1, REACH + 1):
        found = [layer() for at, layer in terms if at == distance]
        if found:
            term = SIDE[distance - 1] * functools.reduce(lambda a, b: a + b, found)
            total = term if total is None else total + term
    return total


def within(at, layers):
    return weighted([(abs(at - i), lambda i=i: layers(i)) for i in range(REACH) if i != at])


def from_other(at, layers):
    last = 2 * REACH - 1
    return weighted([(last - i - at, lambda i=i: layers(i)) for i in range(REACH)])


def across(at, layers):
    return weighted([(at + 1 + i, lambda i=i: layers(i)) for i in range(REACH)])


def add(*values):
    return functools.reduce(lambda a, b: a + b, [v for v in values if v is not None])


def layer_rows(layer, size_y):
    return slice(layer * size_y, (layer + 1) * size_y)


def early_kernel(courant, now, adjoint, packet, speeds, fields, adjoints, sems):
    size_y = fields.shape[1]
    odd = lax.rem(lax.axis_index("space"), 2)
    pairs = ((courant, speeds), (adjoint, adjoints), (now, fields))
    copies = [
        pltpu.make_async_copy(source.at[pl.ds(odd * REACH, REACH)], target, sems.at[number])
        for number, (source, target) in enumerate(pairs)
    ]
    for copy in copies:
        copy.start()
    for copy in copies:
        copy.wait()
    for layer in range(REACH):
        at = layer + odd * (REACH - 1 - 2 * layer)
        speed = speeds[at]
        packet[layer_rows(layer, size_y)] = fields[at]
        packet[layer_rows(REACH + layer, size_y)] = speed * speed * adjoints[at]
        if layer < EARLY_SPEEDS:
            packet[layer_rows(2 * REACH + layer, size_y)] = speed
    packet[(2 * REACH + EARLY_SPEEDS) * size_y :, :] = fields[0, 0:EARLY_EXTRA, :]


def local_kernel(
    sent_first,
    courant,
    now,
    adjoint,
    old,
    late,
    accel,
    adjoint_mid,
    speeds,
    adjoint_now,
    bands,
    early_in,
    late_out,
    late_in,
    present,
    scaled,
    late_held,
    sem,
):
    size_y, size_z = courant.shape[1:]
    odd = lax.rem(lax.axis_index("space"), 2)
    copy = pltpu.make_async_copy(late, late_held, sem)
    copy.start()
    along_y, along_z = band(REACH * size_y, size_y), band(size_z, size_z)
    bands[0] = along_y
    bands[1] = along_z
    places = [placed(layer, half == 0, odd) for half in range(2) for layer in range(REACH)]
    for at, place in enumerate(places):
        speed = courant[place]
        speeds[at] = speed
        adjoint_now[at] = adjoint[place]
        present[at] = now[place]
        scaled[at] = speed * speed * adjoint[place]
    def put_out(layer, value):
        late_out[layer_rows(layer, size_y)] = value

    def put_in(layer, value):
        late_in[layer] = value

    for mine, put in ((0, put_out), (REACH, put_in)):
        other = REACH - mine
        flat = [
            plane_laplace([layers[mine + at] for at in range(REACH)], along_y, along_z)
            for layers in (present, scaled)
        ]
        if mine == 0:
            copy.wait()
        for at in range(REACH):
            place = places[mine + at]
            speed_sq = speeds[mine + at] * speeds[mine + at]
            laplace = add(
                flat[0][at],
                within(at, lambda i: present[mine + i]),
                from_other(at, lambda i: present[other + i]),
            )
            accel[mine + at] = laplace
            put(at, 2.0 * now[place] - old[place] + speed_sq * laplace)
            laplace = add(
                flat[1][at],
                within(at, lambda i: scaled[mine + i]),
                from_other(at, lambda i: scaled[other + i]),
            )
            field = 2.0 * adjoint[place] - late_held[place] + laplace
            adjoint_mid[mine + at] = field
            put(REACH + at, speed_sq * field)
    for layer in range(EARLY_SPEEDS, REACH):
        put_out(2 * REACH + layer - EARLY_SPEEDS, speeds[layer])
    late_out[(3 * REACH - EARLY_SPEEDS) * size_y :, :] = speeds[0, 0:LATE_EXTRA, :]
    for layer in range(REACH):
        early_in[layer] = present[REACH + layer]
        early_in[REACH + layer] = scaled[REACH + layer]
        if layer < INNER_SPEEDS:
            early_in[2 * REACH + layer] = speeds[REACH + layer]
        else:
            late_in[2 * REACH + layer - INNER_SPEEDS] = speeds[REACH + layer]


def next_halo(at, speed, late, own, points):
    speed_sq = speed * speed
    mid = late(at) + speed_sq * (across(at, lambda i: own[i]) + points[at])
    scaled = late(REACH + at) + speed_sq * (
        across(at, lambda i: own[REACH + i]) + points[REACH + at]
    )
    return mid, scaled


def exchange_order(shots, inward):
    if shots == 4:
        return [0] + (INWARD_ORDER if inward else OUTWARD_ORDER)
    return list(range(shots))


def scatter_rows(gradient, outputs, shots, inward):
    rows = gradient.shape[1] // shots
    me = lax.axis_index("shot")
    for number, shift in enumerate(exchange_order(shots, inward)):
        first = pl.multiple_of(jnp.bitwise_xor(me, shift) * rows, rows)
        outputs[number][...] = gradient[:, pl.ds(first, rows), :]


def inner_kernel(
    pulse,
    receiver_x,
    receiver_yz,
    residual,
    own_in,
    speeds,
    accel,
    adjoint_mid,
    late_in,
    late_out,
    adjoint_now,
    bands,
    halo_early,
    halo_late,
    inner,
    outer,
    forward,
    backward,
    points_out,
    marks,
    added,
    points_in,
    mid,
    scaled,
    next_mid,
    next_scaled,
):
    slab = 2 * REACH
    space = lax.axis_index("space")
    odd = lax.rem(space, 2)
    size_y, size_z = own_in.shape[1:]
    along_y, along_z = bands[0], bands[1]
    z_bits = size_z.bit_length() - 1

    def counted(x):
        local = x - space * slab
        return REACH + local + odd * (slab - 1 - 2 * local)

    cells = receiver_yz[...]
    layer = counted(receiver_x[...])
    inside = (layer >= 0) & (layer < 2 * slab)
    wanted = jnp.where(inside, layer * size_y + jnp.right_shift(cells, z_bits), -1)
    count = wanted.shape[1]
    line = lax.broadcasted_iota(jnp.int32, (2 * slab * size_y, count), 0)
    marks[...] = jnp.where(line == wanted, 1.0, 0.0).astype(BF16)
    depth = lax.broadcasted_iota(jnp.int32, (size_z, count), 0)
    hit = depth == jnp.bitwise_and(cells, size_z - 1)

    def received(step, first, last):
        total = None
        for part in three_parts(residual[pl.ds(step, 1), :]):
            spread = jnp.where(hit, part.astype(F32), 0.0).astype(BF16)
            term = lax.dot_general(
                marks[first * size_y : last * size_y],
                spread,
                (((1,), (1,)), ((), ())),
                preferred_element_type=F32,
            )
            total = term if total is None else total + term
        return total.reshape(last - first, size_y, size_z)

    added[0 : 2 * slab] = received(0, 0, 2 * slab)
    added[2 * slab :] = received(1, REACH, REACH + slab)

    rows, columns = grids(size_y, size_z)
    cell = rows * size_z + columns
    source_layer = counted(pulse[:, 2:3].astype(jnp.int32))
    source_cell = pulse[:, 3:4].astype(jnp.int32)

    def fired(step, at):
        spot = jnp.where(source_layer == at, source_cell, -1)
        return jnp.where(cell == spot, pulse[:, step : step + 1], 0.0)

    for at in range(REACH):
        points_out[at] = fired(0, REACH - 1 - at)
        points_out[REACH + at] = added[REACH - 1 - at]
        points_in[at] = fired(0, REACH + slab + at)
        points_in[REACH + at] = added[REACH + slab + at]
        speed = speeds[at]
        fire = fired(0, REACH + at)
        outer[at] = accel[at] + fire
        outer[REACH + at] = adjoint_mid[at] + added[REACH + at]
        outer[2 * REACH + at] = late_out[layer_rows(at, size_y)] + speed * speed * fire
    for at in range(REACH):
        if at < INNER_SPEEDS:
            speed = halo_early[2 * REACH + at]
        else:
            speed = halo_late[2 * REACH + at - INNER_SPEEDS]
        next_mid[at], next_scaled[at] = next_halo(
            at, speed, lambda i: halo_late[i], own_in, points_in
        )
    for at in range(REACH):
        to = REACH + slab - 1 - at
        speed = speeds[REACH + at]
        speed_sq = speed * speed
        extra = across(at, lambda i: halo_early[i]) + fired(0, to)
        adjoint = adjoint_mid[REACH + at] + across(at, lambda i: halo_early[REACH + i]) + added[to]
        inner[at] = accel[REACH + at] + extra
        inner[REACH + at] = adjoint
        mid[at] = late_in[at] + speed_sq * extra
        scaled[at] = speed_sq * adjoint
    flat_mid = plane_laplace([mid[at] for at in range(REACH)], along_y, along_z)
    flat_scaled = plane_laplace([scaled[at] for at in range(REACH)], along_y, along_z)
    for at in range(REACH):
        to = REACH + at
        forward[at] = add(fired(1, to), from_other(at, lambda i: mid[i]))
        backward[at] = add(
            added[2 * slab + at] - adjoint_now[at],
            from_other(at, lambda i: scaled[i]),
        )
        to = REACH + slab - 1 - at
        forward[REACH + at] = add(
            flat_mid[at],
            fired(1, to),
            within(at, lambda i: mid[i]),
            across(at, lambda i: next_mid[i]),
        )
        backward[REACH + at] = add(
            flat_scaled[at],
            added[2 * slab + slab - 1 - at] - adjoint_now[REACH + at],
            2.0 * inner[REACH + at],
            within(at, lambda i: scaled[i]),
            across(at, lambda i: next_scaled[i]),
        )


def middle_kernel(shots, speeds, halo, inner, outer_part, forward, backward, outer, step, *rest):
    outputs, (gradient,) = rest[:shots], rest[shots:]
    size_y = speeds.shape[1]
    for at in range(REACH):
        speed = speeds[at]
        speed_sq = speed * speed
        extra = across(at, lambda i: halo[layer_rows(i, size_y)])
        adjoint = outer_part[REACH + at] + across(at, lambda i: halo[layer_rows(REACH + i, size_y)])
        outer[at] = outer_part[at] + extra
        outer[REACH + at] = adjoint
        step[at] = outer_part[2 * REACH + at] + speed_sq * extra
        step[REACH + at] = speed_sq * adjoint
    for at in range(REACH):
        ahead = add(forward[REACH + at], from_other(at, lambda i: step[i]))
        back = add(backward[REACH + at], from_other(at, lambda i: step[REACH + i]))
        speed = speeds[REACH + at]
        gradient[at] = 2.0 * speed * (back * inner[at] + inner[REACH + at] * ahead)
    scatter_rows(gradient, outputs, shots, True)


def second_kernel(bands, outer, step, forward, backward, after):
    along_y, along_z = bands[0], bands[1]
    flat_mid = plane_laplace([step[at] for at in range(REACH)], along_y, along_z)
    flat_scaled = plane_laplace([step[REACH + at] for at in range(REACH)], along_y, along_z)
    for at in range(REACH):
        after[at] = add(forward[at], flat_mid[at], within(at, lambda i: step[i]))
        after[REACH + at] = add(
            backward[at],
            2.0 * outer[REACH + at],
            flat_scaled[at],
            within(at, lambda i: step[REACH + i]),
        )


def outer_kernel(shots, relayed, own_out, speeds, outer, after, halo_early, points_out, *rest):
    lates, rest = rest[: 1 + relayed], rest[1 + relayed :]
    outputs, (next_mid, next_scaled, gradient) = rest[:shots], rest[shots:]

    def late(layer):
        return add(*[packet[layer_rows(layer, size_y)] for packet in lates])

    size_y = speeds.shape[1]
    own = [own_out[layer_rows(i, size_y)] for i in range(2 * REACH)]
    for at in range(REACH):
        if at < EARLY_SPEEDS:
            speed = halo_early[layer_rows(2 * REACH + at, size_y)]
        else:
            speed = late(2 * REACH + at - EARLY_SPEEDS)
        next_mid[at], next_scaled[at] = next_halo(at, speed, late, own, points_out)
    for at in range(REACH):
        ahead = after[at] + across(at, lambda i: next_mid[i])
        back = after[REACH + at] + across(at, lambda i: next_scaled[i])
        speed = speeds[at]
        gradient[at] = 2.0 * speed * (back * outer[at] + outer[REACH + at] * ahead)
    scatter_rows(gradient, outputs, shots, False)


def add_kernel(*refs):
    refs[-1][...] = functools.reduce(lambda a, b: a + b, [ref[...] for ref in refs[:-1]])


def sum_kernel(inner, *refs):
    outers, out = refs[:-1], refs[-1]
    odd = lax.rem(lax.axis_index("space"), 2)
    for at in range(REACH):
        out[placed(at, True, odd)] = functools.reduce(lambda a, b: a + b, [r[at] for r in outers])
        out[placed(at, False, odd)] = inner[at]


def call(kernel, shapes, in_spaces, scratch, flops, moved):
    def shape(given):
        return jax.ShapeDtypeStruct(given, F32) if isinstance(given, tuple) else given

    many = isinstance(shapes, list)
    return pl.pallas_call(
        kernel,
        out_shape=[shape(s) for s in shapes] if many else shape(shapes),
        in_specs=[pl.BlockSpec(memory_space=space) for space in in_spaces],
        out_specs=[pl.BlockSpec(memory_space=pltpu.VMEM) for _ in shapes]
        if many
        else pl.BlockSpec(memory_space=pltpu.VMEM),
        scratch_shapes=scratch,
        compiler_params=pltpu.CompilerParams(vmem_limit_bytes=VMEM_LIMIT),
        cost_estimate=pl.CostEstimate(flops=flops, bytes_accessed=moved, transcendentals=0),
    )


def both_ways(pairs):
    return pairs + [(b, a) for a, b in pairs]


def on_device(
    courant,
    field_old,
    field_now,
    adjoint_late,
    adjoint_now,
    source_x,
    source_yz,
    wavelet,
    receiver_x,
    receiver_yz,
    residual_trace,
):
    slab, size_y, size_z = courant.shape
    if slab != 2 * REACH:
        raise ValueError("unsupported slab")
    shots = lax.axis_size("shot")
    devices = lax.axis_size("space")
    plane = size_y * size_z
    part_rows = size_y // shots
    V, H = pltpu.VMEM, pltpu.HBM

    def stack(layers):
        return (layers, size_y, size_z)

    def held(layers):
        return pltpu.VMEM(stack(layers), F32)

    def in_hbm(values):
        return pltpu.with_memory_space_constraint(values, pltpu.HBM)

    out_pairs = both_ways([(i, i + 1) for i in range(1, devices - 1, 2)])
    in_pairs = [(i, i ^ 1) for i in range(devices)]
    relayed = devices == 8
    old, now, late, adjoint = (
        field[0] for field in (field_old, field_now, adjoint_late, adjoint_now)
    )
    place = [source_x.astype(F32), source_yz.astype(F32)]
    pulse = jnp.concatenate([wavelet[0]] + place).reshape(1, 4)

    early_layers = 2 * REACH + EARLY_SPEEDS
    late_layers = 3 * REACH - EARLY_SPEEDS
    early_out = call(
        early_kernel,
        (early_layers * size_y + EARLY_EXTRA, size_z),
        [H] * 3,
        [held(REACH)] * 3 + [pltpu.SemaphoreType.DMA((3,))],
        SMALL,
        SMALL,
    )(in_hbm(courant), in_hbm(now), in_hbm(adjoint))
    halo_out = lax.ppermute(early_out, "space", out_pairs)

    bands = jax.ShapeDtypeStruct((2, size_z, size_z), BF16)
    accel, adjoint_mid, speeds, adjoint_half, bands, early_in, late_out, late_in = call(
        local_kernel,
        [stack(slab)] * 4
        + [bands, stack(2 * REACH + INNER_SPEEDS)]
        + [(late_layers * size_y + LATE_EXTRA, size_z)]
        + [stack(3 * REACH - INNER_SPEEDS)],
        [pl.ANY] + [V] * 4 + [H],
        [held(slab)] * 3 + [pltpu.SemaphoreType.DMA(())],
        LARGE,
        SMALL,
    )(early_out, courant, now, adjoint, old, in_hbm(late))
    halo_in = lax.ppermute(early_in, "space", in_pairs)
    halo_late_in = lax.ppermute(late_in, "space", in_pairs)
    if relayed:
        first_hop = lax.ppermute(late_out, "space", [(3, 7), (4, 0)])
        halo_lates = [lax.ppermute(late_out, "space", both_ways([(1, 2), (5, 6)]))]
    else:
        halo_lates = [lax.ppermute(late_out, "space", out_pairs)]
    inner, outer_part, forward, backward, points_out = call(
        inner_kernel,
        [stack(2 * REACH), stack(3 * REACH)] + [stack(2 * REACH)] * 3,
        [V] * 14,
        [
            pltpu.VMEM((2 * slab * size_y, receiver_x.shape[1]), BF16),
            held(3 * slab),
            held(2 * REACH),
        ]
        + [held(REACH)] * 4,
        SMALL,
        SMALL,
    )(
        pulse,
        receiver_x,
        receiver_yz,
        residual_trace[0].T,
        early_in,
        speeds,
        accel,
        adjoint_mid,
        late_in,
        late_out,
        adjoint_half,
        bands,
        halo_in,
        halo_late_in,
    )
    if relayed:
        first_hop, inner = lax.optimization_barrier((first_hop, inner))
        halo_lates.append(lax.ppermute(first_hop, "space", [(7, 4), (0, 3)]))
    outer, step, *inner_parts = call(
        functools.partial(middle_kernel, shots),
        [stack(2 * REACH)] * 2 + [(REACH, part_rows, size_z)] * shots,
        [V] * 6,
        [held(REACH)],
        MIDDLE_COST,
        SMALL,
    )(speeds, halo_out, inner, outer_part, forward, backward)
    after = call(second_kernel, stack(2 * REACH), [V] * 5, [], SECOND_COST, SMALL)(
        bands, outer, step, forward, backward
    )
    shifts = [
        [[(i, i ^ k) for i in range(shots)] for k in exchange_order(shots, inward)]
        for inward in (True, False)
    ]
    inner_parts = inner_parts[:1] + [
        lax.ppermute(inner_parts[k], "shot", shifts[0][k]) for k in range(1, shots)
    ]
    inner_sum = call(add_kernel, (REACH, part_rows, size_z), [V] * shots, [], LARGE, SMALL)(
        *inner_parts
    )
    outer_parts = call(
        functools.partial(outer_kernel, shots, relayed),
        [(REACH, part_rows, size_z)] * shots,
        [V] * (6 + len(halo_lates)),
        [held(REACH)] * 3,
        SMALL,
        SMALL,
    )(early_out, speeds, outer, after, halo_out, points_out, *halo_lates)
    outer_parts = list(outer_parts[:1]) + [
        lax.ppermute(outer_parts[k], "shot", shifts[1][k]) for k in range(1, shots)
    ]
    return call(sum_kernel, (slab, part_rows, size_z), [V] * (1 + shots), [], SMALL, SMALL)(
        inner_sum, *outer_parts
    )


def solution(mesh):
    field = P("shot", "space", None, None)
    specs = (
        P("space", None, None),
        field,
        field,
        field,
        field,
        P("shot"),
        P("shot"),
        P("shot", None),
        P("shot", None),
        P("shot", None),
        P("shot", None, None),
    )
    return jax.shard_map(
        on_device, mesh=mesh, in_specs=specs, out_specs=P("space", "shot", None), check_vma=False
    )
```

```python
import functools
import jax
import jax.numpy as jnp
from jax import lax
from jax.experimental import pallas as pl
from jax.experimental.pallas import tpu as pltpu
from jax.sharding import PartitionSpec as P

MIDDLE = 3.0 * (-205.0 / 72.0)
SIDE = (8.0 / 5.0, -1.0 / 5.0, 8.0 / 315.0, -1.0 / 560.0)
REACH = 4
SCALE = 5040.0
WHOLE_SIDE = (8064.0, -1008.0, 128.0, -9.0)
EARLY_SPEEDS, INNER_SPEEDS = REACH // 2, REACH // 2
EARLY_EXTRA = 8
INWARD_ORDER, OUTWARD_ORDER = [2, 3, 1], [2, 3, 1]
F32 = jnp.float32
BF16 = jnp.bfloat16
VMEM_LIMIT = 32 * 1024 * 1024
MIDDLE_COST = int(8 * 10**9)
SECOND_COST = int(0.001 * 10**9)
SMALL, LARGE = 10**6, 10**10


def placed(layer, outward, odd):
    layer = layer if outward else 2 * REACH - 1 - layer
    return layer + odd * (2 * REACH - 1 - 2 * layer)


def grids(size_y, size_z):
    rows = lax.broadcasted_iota(jnp.int32, (size_y, size_z), 0)
    columns = lax.broadcasted_iota(jnp.int32, (size_y, size_z), 1)
    return rows, columns


def three_parts(values):
    high = values.astype(BF16)
    rest = values - high.astype(F32)
    middle = rest.astype(BF16)
    return high, middle, (rest - middle.astype(F32)).astype(BF16)


def band(size, block):
    rows, columns = grids(size, size)
    distance = jnp.abs(rows - columns)
    weights = jnp.zeros((size, size), F32)
    for offset in range(1, REACH + 1):
        weights = jnp.where(distance == offset, WHOLE_SIDE[offset - 1], weights)
    bits = block.bit_length() - 1
    same = jnp.right_shift(rows, bits) == jnp.right_shift(columns, bits)
    return jnp.where(same, weights, 0.0).astype(BF16)


def plane_laplace(layers, along_y, along_z):
    shape = (len(layers),) + layers[0].shape
    values = jnp.concatenate(layers, axis=0)
    total = None
    for part in three_parts(values)[::-1]:
        term = jnp.dot(part, along_z, preferred_element_type=F32)
        term += jnp.dot(along_y, part, preferred_element_type=F32)
        total = term if total is None else total + term
    return (total * (1.0 / SCALE) + MIDDLE * values).reshape(shape)


def weighted(terms):
    total = None
    for distance in range(1, REACH + 1):
        found = [layer() for at, layer in terms if at == distance]
        if found:
            term = SIDE[distance - 1] * functools.reduce(lambda a, b: a + b, found)
            total = term if total is None else total + term
    return total


def within(at, layers):
    return weighted([(abs(at - i), lambda i=i: layers(i)) for i in range(REACH) if i != at])


def from_other(at, layers):
    last = 2 * REACH - 1
    return weighted([(last - i - at, lambda i=i: layers(i)) for i in range(REACH)])


def across(at, layers):
    return weighted([(at + 1 + i, lambda i=i: layers(i)) for i in range(REACH)])


def add(*values):
    return functools.reduce(lambda a, b: a + b, [v for v in values if v is not None])


def layer_rows(layer, size_y):
    return slice(layer * size_y, (layer + 1) * size_y)


def early_kernel(courant, now, adjoint, packet, speeds, fields, adjoints, sems):
    size_y = fields.shape[1]
    odd = lax.rem(lax.axis_index("space"), 2)
    pairs = ((courant, speeds), (adjoint, adjoints), (now, fields))
    copies = [
        pltpu.make_async_copy(source.at[pl.ds(odd * REACH, REACH)], target, sems.at[number])
        for number, (source, target) in enumerate(pairs)
    ]
    for copy in copies:
        copy.start()
    for copy in copies:
        copy.wait()
    for layer in range(REACH):
        at = layer + odd * (REACH - 1 - 2 * layer)
        speed = speeds[at]
        packet[layer_rows(layer, size_y)] = fields[at]
        packet[layer_rows(REACH + layer, size_y)] = speed * speed * adjoints[at]
    parity = lax.rem(lax.axis_index("shot"), 2)
    for number in range(EARLY_SPEEDS):
        layer = parity * EARLY_SPEEDS + number
        at = layer + odd * (REACH - 1 - 2 * layer)
        packet[layer_rows(2 * REACH + number, size_y)] = speeds[at]
    packet[(2 * REACH + EARLY_SPEEDS) * size_y :, :] = fields[0, 0:EARLY_EXTRA, :]


def local_kernel(
    sent_first,
    courant,
    now,
    adjoint,
    old,
    late,
    accel,
    adjoint_mid,
    speeds,
    adjoint_now,
    bands,
    early_in,
    late_out,
    late_in,
    present,
    scaled,
    late_held,
    sem,
):
    size_y, size_z = courant.shape[1:]
    odd = lax.rem(lax.axis_index("space"), 2)
    copy = pltpu.make_async_copy(late, late_held, sem)
    copy.start()
    along_y, along_z = band(REACH * size_y, size_y), band(size_z, size_z)
    bands[0] = along_y
    bands[1] = along_z
    places = [placed(layer, half == 0, odd) for half in range(2) for layer in range(REACH)]
    for at, place in enumerate(places):
        speed = courant[place]
        speeds[at] = speed
        adjoint_now[at] = adjoint[place]
        present[at] = now[place]
        scaled[at] = speed * speed * adjoint[place]
    def put_out(layer, value):
        late_out[layer_rows(layer, size_y)] = value

    def put_in(layer, value):
        late_in[layer] = value

    for mine, put in ((0, put_out), (REACH, put_in)):
        other = REACH - mine
        flat = [
            plane_laplace([layers[mine + at] for at in range(REACH)], along_y, along_z)
            for layers in (present, scaled)
        ]
        if mine == 0:
            copy.wait()
        for at in range(REACH):
            place = places[mine + at]
            speed_sq = speeds[mine + at] * speeds[mine + at]
            laplace = add(
                flat[0][at],
                within(at, lambda i: present[mine + i]),
                from_other(at, lambda i: present[other + i]),
            )
            accel[mine + at] = laplace
            put(at, 2.0 * now[place] - old[place] + speed_sq * laplace)
            laplace = add(
                flat[1][at],
                within(at, lambda i: scaled[mine + i]),
                from_other(at, lambda i: scaled[other + i]),
            )
            field = 2.0 * adjoint[place] - late_held[place] + laplace
            adjoint_mid[mine + at] = field
            put(REACH + at, speed_sq * field)
    for layer in range(REACH):
        early_in[layer] = present[REACH + layer]
        early_in[REACH + layer] = scaled[REACH + layer]
        if layer < INNER_SPEEDS:
            early_in[2 * REACH + layer] = speeds[REACH + layer]
        else:
            late_in[2 * REACH + layer - INNER_SPEEDS] = speeds[REACH + layer]


def next_halo(at, speed, late, own, points):
    speed_sq = speed * speed
    mid = late(at) + speed_sq * (across(at, lambda i: own[i]) + points[at])
    scaled = late(REACH + at) + speed_sq * (
        across(at, lambda i: own[REACH + i]) + points[REACH + at]
    )
    return mid, scaled


def exchange_order(shots, inward):
    if shots == 4:
        return [0] + (INWARD_ORDER if inward else OUTWARD_ORDER)
    return list(range(shots))


def scatter_rows(gradient, outputs, shots, inward):
    rows = gradient.shape[1] // shots
    me = lax.axis_index("shot")
    for number, shift in enumerate(exchange_order(shots, inward)):
        first = pl.multiple_of(jnp.bitwise_xor(me, shift) * rows, rows)
        outputs[number][...] = gradient[:, pl.ds(first, rows), :]


def inner_kernel(
    pulse,
    receiver_x,
    receiver_yz,
    residual,
    own_in,
    speeds,
    accel,
    adjoint_mid,
    late_in,
    late_out,
    adjoint_now,
    bands,
    halo_early,
    halo_late,
    inner,
    outer,
    forward,
    backward,
    points_out,
    marks,
    added,
    points_in,
    mid,
    scaled,
    next_mid,
    next_scaled,
):
    slab = 2 * REACH
    space = lax.axis_index("space")
    odd = lax.rem(space, 2)
    size_y, size_z = own_in.shape[1:]
    along_y, along_z = bands[0], bands[1]
    z_bits = size_z.bit_length() - 1

    def counted(x):
        local = x - space * slab
        return REACH + local + odd * (slab - 1 - 2 * local)

    cells = receiver_yz[...]
    layer = counted(receiver_x[...])
    inside = (layer >= 0) & (layer < 2 * slab)
    wanted = jnp.where(inside, layer * size_y + jnp.right_shift(cells, z_bits), -1)
    count = wanted.shape[1]
    line = lax.broadcasted_iota(jnp.int32, (2 * slab * size_y, count), 0)
    marks[...] = jnp.where(line == wanted, 1.0, 0.0).astype(BF16)
    depth = lax.broadcasted_iota(jnp.int32, (size_z, count), 0)
    hit = depth == jnp.bitwise_and(cells, size_z - 1)

    def received(step, first, last):
        total = None
        for part in three_parts(residual[pl.ds(step, 1), :]):
            spread = jnp.where(hit, part.astype(F32), 0.0).astype(BF16)
            term = lax.dot_general(
                marks[first * size_y : last * size_y],
                spread,
                (((1,), (1,)), ((), ())),
                preferred_element_type=F32,
            )
            total = term if total is None else total + term
        return total.reshape(last - first, size_y, size_z)

    added[0 : 2 * slab] = received(0, 0, 2 * slab)
    added[2 * slab :] = received(1, REACH, REACH + slab)

    rows, columns = grids(size_y, size_z)
    cell = rows * size_z + columns
    source_layer = counted(pulse[:, 2:3].astype(jnp.int32))
    source_cell = pulse[:, 3:4].astype(jnp.int32)

    def fired(step, at):
        spot = jnp.where(source_layer == at, source_cell, -1)
        return jnp.where(cell == spot, pulse[:, step : step + 1], 0.0)

    for at in range(REACH):
        points_out[at] = fired(0, REACH - 1 - at)
        points_out[REACH + at] = added[REACH - 1 - at]
        points_in[at] = fired(0, REACH + slab + at)
        points_in[REACH + at] = added[REACH + slab + at]
        speed = speeds[at]
        fire = fired(0, REACH + at)
        outer[at] = accel[at] + fire
        outer[REACH + at] = adjoint_mid[at] + added[REACH + at]
        outer[2 * REACH + at] = late_out[layer_rows(at, size_y)] + speed * speed * fire
    for at in range(REACH):
        if at < INNER_SPEEDS:
            speed = halo_early[2 * REACH + at]
        else:
            speed = halo_late[2 * REACH + at - INNER_SPEEDS]
        next_mid[at], next_scaled[at] = next_halo(
            at, speed, lambda i: halo_late[i], own_in, points_in
        )
    for at in range(REACH):
        to = REACH + slab - 1 - at
        speed = speeds[REACH + at]
        speed_sq = speed * speed
        extra = across(at, lambda i: halo_early[i]) + fired(0, to)
        adjoint = adjoint_mid[REACH + at] + across(at, lambda i: halo_early[REACH + i]) + added[to]
        inner[at] = accel[REACH + at] + extra
        inner[REACH + at] = adjoint
        mid[at] = late_in[at] + speed_sq * extra
        scaled[at] = speed_sq * adjoint
    flat_mid = plane_laplace([mid[at] for at in range(REACH)], along_y, along_z)
    flat_scaled = plane_laplace([scaled[at] for at in range(REACH)], along_y, along_z)
    for at in range(REACH):
        to = REACH + at
        forward[at] = add(fired(1, to), from_other(at, lambda i: mid[i]))
        backward[at] = add(
            added[2 * slab + at] - adjoint_now[at],
            from_other(at, lambda i: scaled[i]),
        )
        to = REACH + slab - 1 - at
        forward[REACH + at] = add(
            flat_mid[at],
            fired(1, to),
            within(at, lambda i: mid[i]),
            across(at, lambda i: next_mid[i]),
        )
        backward[REACH + at] = add(
            flat_scaled[at],
            added[2 * slab + slab - 1 - at] - adjoint_now[REACH + at],
            2.0 * inner[REACH + at],
            within(at, lambda i: scaled[i]),
            across(at, lambda i: next_scaled[i]),
        )


def middle_kernel(shots, speeds, halo, inner, outer_part, forward, backward, outer, step, *rest):
    shared, outputs, (gradient,) = rest[0], rest[1 : 1 + shots], rest[1 + shots :]
    size_y = speeds.shape[1]
    for at in range(REACH):
        speed = speeds[at]
        speed_sq = speed * speed
        extra = across(at, lambda i: halo[layer_rows(i, size_y)])
        adjoint = outer_part[REACH + at] + across(at, lambda i: halo[layer_rows(REACH + i, size_y)])
        outer[at] = outer_part[at] + extra
        outer[REACH + at] = adjoint
        step[at] = outer_part[2 * REACH + at] + speed_sq * extra
        step[REACH + at] = speed_sq * adjoint
    for at in range(REACH):
        ahead = add(forward[REACH + at], from_other(at, lambda i: step[i]))
        back = add(backward[REACH + at], from_other(at, lambda i: step[REACH + i]))
        speed = speeds[REACH + at]
        gradient[at] = 2.0 * speed * (back * inner[at] + inner[REACH + at] * ahead)
    scatter_rows(gradient, outputs, shots, True)
    for number in range(EARLY_SPEEDS):
        shared[number] = halo[layer_rows(2 * REACH + number, size_y)]


def second_kernel(bands, outer, step, forward, backward, after):
    along_y, along_z = bands[0], bands[1]
    flat_mid = plane_laplace([step[at] for at in range(REACH)], along_y, along_z)
    flat_scaled = plane_laplace([step[REACH + at] for at in range(REACH)], along_y, along_z)
    for at in range(REACH):
        after[at] = add(forward[at], flat_mid[at], within(at, lambda i: step[i]))
        after[REACH + at] = add(
            backward[at],
            2.0 * outer[REACH + at],
            flat_scaled[at],
            within(at, lambda i: step[REACH + i]),
        )


def outer_kernel(
    shots, relayed, own_out, speeds, outer, after, shared, passed, points_out, *rest
):
    lates, rest = rest[: 1 + relayed], rest[1 + relayed :]
    outputs, (next_mid, next_scaled, gradient) = rest[:shots], rest[shots:]

    def late(layer):
        return add(*[packet[layer_rows(layer, size_y)] for packet in lates])

    size_y = speeds.shape[1]
    own = [own_out[layer_rows(i, size_y)] for i in range(2 * REACH)]
    parity = lax.rem(lax.axis_index("shot"), 2)
    for at in range(REACH):
        mine, number = parity == at // EARLY_SPEEDS, at % EARLY_SPEEDS
        speed = jnp.where(mine, shared[number], passed[number])
        next_mid[at], next_scaled[at] = next_halo(at, speed, late, own, points_out)
    for at in range(REACH):
        ahead = after[at] + across(at, lambda i: next_mid[i])
        back = after[REACH + at] + across(at, lambda i: next_scaled[i])
        speed = speeds[at]
        gradient[at] = 2.0 * speed * (back * outer[at] + outer[REACH + at] * ahead)
    scatter_rows(gradient, outputs, shots, False)


def add_kernel(*refs):
    refs[-1][...] = functools.reduce(lambda a, b: a + b, [ref[...] for ref in refs[:-1]])


def sum_kernel(inner, inner_near, *refs):
    outers, out = refs[:-1], refs[-1]
    odd = lax.rem(lax.axis_index("space"), 2)
    for at in range(REACH):
        out[placed(at, True, odd)] = functools.reduce(lambda a, b: a + b, [r[at] for r in outers])
        out[placed(at, False, odd)] = inner[at] + inner_near[at]


def call(kernel, shapes, in_spaces, scratch, flops, moved):
    def shape(given):
        return jax.ShapeDtypeStruct(given, F32) if isinstance(given, tuple) else given

    many = isinstance(shapes, list)
    return pl.pallas_call(
        kernel,
        out_shape=[shape(s) for s in shapes] if many else shape(shapes),
        in_specs=[pl.BlockSpec(memory_space=space) for space in in_spaces],
        out_specs=[pl.BlockSpec(memory_space=pltpu.VMEM) for _ in shapes]
        if many
        else pl.BlockSpec(memory_space=pltpu.VMEM),
        scratch_shapes=scratch,
        compiler_params=pltpu.CompilerParams(vmem_limit_bytes=VMEM_LIMIT),
        cost_estimate=pl.CostEstimate(flops=flops, bytes_accessed=moved, transcendentals=0),
    )


def both_ways(pairs):
    return pairs + [(b, a) for a, b in pairs]


def on_device(
    courant,
    field_old,
    field_now,
    adjoint_late,
    adjoint_now,
    source_x,
    source_yz,
    wavelet,
    receiver_x,
    receiver_yz,
    residual_trace,
):
    slab, size_y, size_z = courant.shape
    shots = lax.axis_size("shot")
    if slab != 2 * REACH or shots % 2:
        raise ValueError("unsupported slab")
    devices = lax.axis_size("space")
    plane = size_y * size_z
    part_rows = size_y // shots
    V, H = pltpu.VMEM, pltpu.HBM

    def stack(layers):
        return (layers, size_y, size_z)

    def held(layers):
        return pltpu.VMEM(stack(layers), F32)

    def in_hbm(values):
        return pltpu.with_memory_space_constraint(values, pltpu.HBM)

    out_pairs = both_ways([(i, i + 1) for i in range(1, devices - 1, 2)])
    in_pairs = [(i, i ^ 1) for i in range(devices)]
    relayed = devices == 8
    old, now, late, adjoint = (
        field[0] for field in (field_old, field_now, adjoint_late, adjoint_now)
    )
    place = [source_x.astype(F32), source_yz.astype(F32)]
    pulse = jnp.concatenate([wavelet[0]] + place).reshape(1, 4)

    early_layers = 2 * REACH + EARLY_SPEEDS
    early_out = call(
        early_kernel,
        (early_layers * size_y + EARLY_EXTRA, size_z),
        [H] * 3,
        [held(REACH)] * 3 + [pltpu.SemaphoreType.DMA((3,))],
        SMALL,
        SMALL,
    )(in_hbm(courant), in_hbm(now), in_hbm(adjoint))
    halo_out = lax.ppermute(early_out, "space", out_pairs)

    bands = jax.ShapeDtypeStruct((2, size_z, size_z), BF16)
    accel, adjoint_mid, speeds, adjoint_half, bands, early_in, late_out, late_in = call(
        local_kernel,
        [stack(slab)] * 4
        + [bands, stack(2 * REACH + INNER_SPEEDS)]
        + [(2 * REACH * size_y, size_z)]
        + [stack(3 * REACH - INNER_SPEEDS)],
        [pl.ANY] + [V] * 4 + [H],
        [held(slab)] * 3 + [pltpu.SemaphoreType.DMA(())],
        LARGE,
        SMALL,
    )(early_out, courant, now, adjoint, old, in_hbm(late))
    halo_in = lax.ppermute(early_in, "space", in_pairs)
    halo_late_in = lax.ppermute(late_in, "space", in_pairs)
    if relayed:
        first_hop = lax.ppermute(late_out, "space", [(3, 7), (4, 0)])
        halo_lates = [lax.ppermute(late_out, "space", both_ways([(1, 2), (5, 6)]))]
    else:
        halo_lates = [lax.ppermute(late_out, "space", out_pairs)]
    inner, outer_part, forward, backward, points_out = call(
        inner_kernel,
        [stack(2 * REACH), stack(3 * REACH)] + [stack(2 * REACH)] * 3,
        [V] * 14,
        [
            pltpu.VMEM((2 * slab * size_y, receiver_x.shape[1]), BF16),
            held(3 * slab),
            held(2 * REACH),
        ]
        + [held(REACH)] * 4,
        SMALL,
        SMALL,
    )(
        pulse,
        receiver_x,
        receiver_yz,
        residual_trace[0].T,
        early_in,
        speeds,
        accel,
        adjoint_mid,
        late_in,
        late_out,
        adjoint_half,
        bands,
        halo_in,
        halo_late_in,
    )
    if relayed:
        first_hop, inner = lax.optimization_barrier((first_hop, inner))
        halo_lates.append(lax.ppermute(first_hop, "space", [(7, 4), (0, 3)]))
    outer, step, shared, *inner_parts = call(
        functools.partial(middle_kernel, shots),
        [stack(2 * REACH)] * 2 + [stack(EARLY_SPEEDS)] + [(REACH, part_rows, size_z)] * shots,
        [V] * 6,
        [held(REACH)],
        MIDDLE_COST,
        SMALL,
    )(speeds, halo_out, inner, outer_part, forward, backward)
    after = call(second_kernel, stack(2 * REACH), [V] * 5, [], SECOND_COST, SMALL)(
        bands, outer, step, forward, backward
    )
    passed = lax.ppermute(shared, "shot", [(i, i ^ 1) for i in range(shots)])

    def exchanged(part, shift):
        return lax.ppermute(part, "shot", [(i, i ^ shift) for i in range(shots)])

    order = exchange_order(shots, True)
    inner_near = inner_parts[order.index(1)]
    early_parts = [
        exchanged(part, shift) if shift else part
        for part, shift in zip(inner_parts, order)
        if shift != 1
    ]
    inner_sum = call(
        add_kernel, (REACH, part_rows, size_z), [V] * (shots - 1), [], LARGE, SMALL
    )(*early_parts)
    order = exchange_order(shots, False)
    outer_parts = call(
        functools.partial(outer_kernel, shots, relayed),
        [(REACH, part_rows, size_z)] * shots,
        [V] * (7 + len(halo_lates)),
        [held(REACH)] * 3,
        SMALL,
        SMALL,
    )(early_out, speeds, outer, after, shared, passed, points_out, *halo_lates)
    inner_near, *outer_parts = lax.optimization_barrier((inner_near, *outer_parts))
    inner_near = exchanged(inner_near, 1)
    outer_parts = [
        exchanged(part, shift) if shift else part for part, shift in zip(outer_parts, order)
    ]
    return call(
        sum_kernel,
        (slab, part_rows, size_z),
        [V] * (2 + shots),
        [],
        SMALL,
        SMALL,
    )(inner_sum, inner_near, *outer_parts)


def solution(mesh):
    field = P("shot", "space", None, None)
    specs = (
        P("space", None, None),
        field,
        field,
        field,
        field,
        P("shot"),
        P("shot"),
        P("shot", None),
        P("shot", None),
        P("shot", None),
        P("shot", None, None),
    )
    return jax.shard_map(
        on_device, mesh=mesh, in_specs=specs, out_specs=P("space", "shot", None), check_vma=False
    )
```

```python
import functools
import jax
import jax.numpy as jnp
from jax import lax
from jax.experimental import pallas as pl
from jax.experimental.pallas import tpu as pltpu
from jax.sharding import PartitionSpec as P

MIDDLE = 3.0 * (-205.0 / 72.0)
SIDE = (8.0 / 5.0, -1.0 / 5.0, 8.0 / 315.0, -1.0 / 560.0)
REACH = 4
SCALE = 5040.0
WHOLE_SIDE = (8064.0, -1008.0, 128.0, -9.0)
EARLY_SPEEDS, INNER_SPEEDS = REACH // 2, REACH // 2
EARLY_EXTRA = 8
INWARD_ORDER, OUTWARD_ORDER = [2, 3, 1], [2, 3, 1]
F32 = jnp.float32
BF16 = jnp.bfloat16
VMEM_LIMIT = 32 * 1024 * 1024
MIDDLE_COST = int(8 * 10**9)
SECOND_COST = int(0.001 * 10**9)
SMALL, LARGE = 10**6, 10**10


def placed(layer, outward, odd):
    layer = layer if outward else 2 * REACH - 1 - layer
    return layer + odd * (2 * REACH - 1 - 2 * layer)


def grids(size_y, size_z):
    rows = lax.broadcasted_iota(jnp.int32, (size_y, size_z), 0)
    columns = lax.broadcasted_iota(jnp.int32, (size_y, size_z), 1)
    return rows, columns


def three_parts(values):
    high = values.astype(BF16)
    rest = values - high.astype(F32)
    middle = rest.astype(BF16)
    return high, middle, (rest - middle.astype(F32)).astype(BF16)


def band(size, block):
    rows, columns = grids(size, size)
    distance = jnp.abs(rows - columns)
    weights = jnp.zeros((size, size), F32)
    for offset in range(1, REACH + 1):
        weights = jnp.where(distance == offset, WHOLE_SIDE[offset - 1], weights)
    bits = block.bit_length() - 1
    same = jnp.right_shift(rows, bits) == jnp.right_shift(columns, bits)
    return jnp.where(same, weights, 0.0).astype(BF16)


def plane_laplace(layers, along_y, along_z):
    shape = (len(layers),) + layers[0].shape
    values = jnp.concatenate(layers, axis=0)
    total = None
    for part in three_parts(values)[::-1]:
        term = jnp.dot(part, along_z, preferred_element_type=F32)
        term += jnp.dot(along_y, part, preferred_element_type=F32)
        total = term if total is None else total + term
    return (total * (1.0 / SCALE) + MIDDLE * values).reshape(shape)


def weighted(terms):
    total = None
    for distance in range(1, REACH + 1):
        found = [layer() for at, layer in terms if at == distance]
        if found:
            term = SIDE[distance - 1] * functools.reduce(lambda a, b: a + b, found)
            total = term if total is None else total + term
    return total


def within(at, layers):
    return weighted([(abs(at - i), lambda i=i: layers(i)) for i in range(REACH) if i != at])


def from_other(at, layers):
    last = 2 * REACH - 1
    return weighted([(last - i - at, lambda i=i: layers(i)) for i in range(REACH)])


def across(at, layers):
    return weighted([(at + 1 + i, lambda i=i: layers(i)) for i in range(REACH)])


def add(*values):
    return functools.reduce(lambda a, b: a + b, [v for v in values if v is not None])


def layer_rows(layer, size_y):
    return slice(layer * size_y, (layer + 1) * size_y)


def early_kernel(courant, now, adjoint, packet, speeds, fields, adjoints, sems):
    size_y = fields.shape[1]
    odd = lax.rem(lax.axis_index("space"), 2)
    pairs = ((courant, speeds), (adjoint, adjoints), (now, fields))
    copies = [
        pltpu.make_async_copy(source.at[pl.ds(odd * REACH, REACH)], target, sems.at[number])
        for number, (source, target) in enumerate(pairs)
    ]
    for copy in copies:
        copy.start()
    for copy in copies:
        copy.wait()
    for layer in range(REACH):
        at = layer + odd * (REACH - 1 - 2 * layer)
        speed = speeds[at]
        packet[layer_rows(layer, size_y)] = fields[at]
        packet[layer_rows(REACH + layer, size_y)] = speed * speed * adjoints[at]
    parity = lax.rem(lax.axis_index("shot"), 2)
    for number in range(EARLY_SPEEDS):
        layer = parity * EARLY_SPEEDS + number
        at = layer + odd * (REACH - 1 - 2 * layer)
        packet[layer_rows(2 * REACH + number, size_y)] = speeds[at]
    packet[(2 * REACH + EARLY_SPEEDS) * size_y :, :] = fields[0, 0:EARLY_EXTRA, :]


def local_kernel(
    sent_first,
    courant,
    now,
    adjoint,
    old,
    late,
    accel,
    adjoint_mid,
    speeds,
    adjoint_now,
    bands,
    early_in,
    late_out,
    late_in,
    present,
    scaled,
    late_held,
    sem,
):
    size_y, size_z = courant.shape[1:]
    odd = lax.rem(lax.axis_index("space"), 2)
    copy = pltpu.make_async_copy(late, late_held, sem)
    copy.start()
    along_y, along_z = band(REACH * size_y, size_y), band(size_z, size_z)
    bands[0] = along_y
    bands[1] = along_z
    places = [placed(layer, half == 0, odd) for half in range(2) for layer in range(REACH)]
    for at, place in enumerate(places):
        speed = courant[place]
        speeds[at] = speed
        adjoint_now[at] = adjoint[place]
        present[at] = now[place]
        scaled[at] = speed * speed * adjoint[place]
    def put_out(layer, value):
        late_out[layer_rows(layer, size_y)] = value

    def put_in(layer, value):
        late_in[layer] = value

    for mine, put in ((0, put_out), (REACH, put_in)):
        other = REACH - mine
        flat = [
            plane_laplace([layers[mine + at] for at in range(REACH)], along_y, along_z)
            for layers in (present, scaled)
        ]
        if mine == 0:
            copy.wait()
        for at in range(REACH):
            place = places[mine + at]
            speed_sq = speeds[mine + at] * speeds[mine + at]
            laplace = add(
                flat[0][at],
                within(at, lambda i: present[mine + i]),
                from_other(at, lambda i: present[other + i]),
            )
            accel[mine + at] = laplace
            put(at, 2.0 * now[place] - old[place] + speed_sq * laplace)
            laplace = add(
                flat[1][at],
                within(at, lambda i: scaled[mine + i]),
                from_other(at, lambda i: scaled[other + i]),
            )
            field = 2.0 * adjoint[place] - late_held[place] + laplace
            adjoint_mid[mine + at] = field
            put(REACH + at, speed_sq * field)
    for layer in range(REACH):
        early_in[layer] = present[REACH + layer]
        early_in[REACH + layer] = scaled[REACH + layer]
        if layer < INNER_SPEEDS:
            early_in[2 * REACH + layer] = speeds[REACH + layer]
        else:
            late_in[2 * REACH + layer - INNER_SPEEDS] = speeds[REACH + layer]


def next_halo(at, speed, late, own, points):
    speed_sq = speed * speed
    mid = late(at) + speed_sq * (across(at, lambda i: own[i]) + points[at])
    scaled = late(REACH + at) + speed_sq * (
        across(at, lambda i: own[REACH + i]) + points[REACH + at]
    )
    return mid, scaled


def exchange_order(shots, inward):
    if shots == 4:
        return [0] + (INWARD_ORDER if inward else OUTWARD_ORDER)
    return list(range(shots))


def scatter_rows(gradient, outputs, shots, inward):
    rows = gradient.shape[1] // shots
    me = lax.axis_index("shot")
    for number, shift in enumerate(exchange_order(shots, inward)):
        first = pl.multiple_of(jnp.bitwise_xor(me, shift) * rows, rows)
        outputs[number][...] = gradient[:, pl.ds(first, rows), :]


def inner_kernel(
    pulse,
    receiver_x,
    receiver_yz,
    residual,
    own_in,
    speeds,
    accel,
    adjoint_mid,
    late_in,
    late_out,
    adjoint_now,
    bands,
    halo_early,
    halo_late,
    inner,
    outer,
    forward,
    backward,
    points_out,
    marks,
    added,
    points_in,
    mid,
    scaled,
    next_mid,
    next_scaled,
):
    slab = 2 * REACH
    space = lax.axis_index("space")
    odd = lax.rem(space, 2)
    size_y, size_z = own_in.shape[1:]
    along_y, along_z = bands[0], bands[1]
    z_bits = size_z.bit_length() - 1

    def counted(x):
        local = x - space * slab
        return REACH + local + odd * (slab - 1 - 2 * local)

    cells = receiver_yz[...]
    layer = counted(receiver_x[...])
    inside = (layer >= 0) & (layer < 2 * slab)
    wanted = jnp.where(inside, layer * size_y + jnp.right_shift(cells, z_bits), -1)
    count = wanted.shape[1]
    line = lax.broadcasted_iota(jnp.int32, (2 * slab * size_y, count), 0)
    marks[...] = jnp.where(line == wanted, 1.0, 0.0).astype(BF16)
    depth = lax.broadcasted_iota(jnp.int32, (size_z, count), 0)
    hit = depth == jnp.bitwise_and(cells, size_z - 1)

    def received(step, first, last):
        total = None
        for part in three_parts(residual[pl.ds(step, 1), :]):
            spread = jnp.where(hit, part.astype(F32), 0.0).astype(BF16)
            term = lax.dot_general(
                marks[first * size_y : last * size_y],
                spread,
                (((1,), (1,)), ((), ())),
                preferred_element_type=F32,
            )
            total = term if total is None else total + term
        return total.reshape(last - first, size_y, size_z)

    added[0 : 2 * slab] = received(0, 0, 2 * slab)
    added[2 * slab :] = received(1, REACH, REACH + slab)

    rows, columns = grids(size_y, size_z)
    cell = rows * size_z + columns
    source_layer = counted(pulse[:, 2:3].astype(jnp.int32))
    source_cell = pulse[:, 3:4].astype(jnp.int32)

    def fired(step, at):
        spot = jnp.where(source_layer == at, source_cell, -1)
        return jnp.where(cell == spot, pulse[:, step : step + 1], 0.0)

    for at in range(REACH):
        points_out[at] = fired(0, REACH - 1 - at)
        points_out[REACH + at] = added[REACH - 1 - at]
        points_in[at] = fired(0, REACH + slab + at)
        points_in[REACH + at] = added[REACH + slab + at]
        speed = speeds[at]
        fire = fired(0, REACH + at)
        outer[at] = accel[at] + fire
        outer[REACH + at] = adjoint_mid[at] + added[REACH + at]
        outer[2 * REACH + at] = late_out[layer_rows(at, size_y)] + speed * speed * fire
    for at in range(REACH):
        if at < INNER_SPEEDS:
            speed = halo_early[2 * REACH + at]
        else:
            speed = halo_late[2 * REACH + at - INNER_SPEEDS]
        next_mid[at], next_scaled[at] = next_halo(
            at, speed, lambda i: halo_late[i], own_in, points_in
        )
    for at in range(REACH):
        to = REACH + slab - 1 - at
        speed = speeds[REACH + at]
        speed_sq = speed * speed
        extra = across(at, lambda i: halo_early[i]) + fired(0, to)
        adjoint = adjoint_mid[REACH + at] + across(at, lambda i: halo_early[REACH + i]) + added[to]
        inner[at] = accel[REACH + at] + extra
        inner[REACH + at] = adjoint
        mid[at] = late_in[at] + speed_sq * extra
        scaled[at] = speed_sq * adjoint
    flat_mid = plane_laplace([mid[at] for at in range(REACH)], along_y, along_z)
    flat_scaled = plane_laplace([scaled[at] for at in range(REACH)], along_y, along_z)
    for at in range(REACH):
        to = REACH + at
        forward[at] = add(fired(1, to), from_other(at, lambda i: mid[i]))
        backward[at] = add(
            added[2 * slab + at] - adjoint_now[at],
            from_other(at, lambda i: scaled[i]),
        )
        to = REACH + slab - 1 - at
        forward[REACH + at] = add(
            flat_mid[at],
            fired(1, to),
            within(at, lambda i: mid[i]),
            across(at, lambda i: next_mid[i]),
        )
        backward[REACH + at] = add(
            flat_scaled[at],
            added[2 * slab + slab - 1 - at] - adjoint_now[REACH + at],
            2.0 * inner[REACH + at],
            within(at, lambda i: scaled[i]),
            across(at, lambda i: next_scaled[i]),
        )


def middle_kernel(shots, speeds, halo, inner, outer_part, forward, backward, outer, step, *rest):
    shared, outputs, (gradient,) = rest[0], rest[1 : 1 + shots], rest[1 + shots :]
    size_y = speeds.shape[1]
    for at in range(REACH):
        speed = speeds[at]
        speed_sq = speed * speed
        extra = across(at, lambda i: halo[layer_rows(i, size_y)])
        adjoint = outer_part[REACH + at] + across(at, lambda i: halo[layer_rows(REACH + i, size_y)])
        outer[at] = outer_part[at] + extra
        outer[REACH + at] = adjoint
        step[at] = outer_part[2 * REACH + at] + speed_sq * extra
        step[REACH + at] = speed_sq * adjoint
    for at in range(REACH):
        ahead = add(forward[REACH + at], from_other(at, lambda i: step[i]))
        back = add(backward[REACH + at], from_other(at, lambda i: step[REACH + i]))
        speed = speeds[REACH + at]
        gradient[at] = 2.0 * speed * (back * inner[at] + inner[REACH + at] * ahead)
    scatter_rows(gradient, outputs, shots, True)
    for number in range(EARLY_SPEEDS):
        shared[number] = halo[layer_rows(2 * REACH + number, size_y)]


def second_kernel(bands, outer, step, forward, backward, after):
    along_y, along_z = bands[0], bands[1]
    flat_mid = plane_laplace([step[at] for at in range(REACH)], along_y, along_z)
    flat_scaled = plane_laplace([step[REACH + at] for at in range(REACH)], along_y, along_z)
    for at in range(REACH):
        after[at] = add(forward[at], flat_mid[at], within(at, lambda i: step[i]))
        after[REACH + at] = add(
            backward[at],
            2.0 * outer[REACH + at],
            flat_scaled[at],
            within(at, lambda i: step[REACH + i]),
        )


def outer_kernel(
    shots, relayed, own_out, speeds, outer, after, shared, passed, points_out, *rest
):
    lates, rest = rest[: 1 + relayed], rest[1 + relayed :]
    outputs, (next_mid, next_scaled, gradient) = rest[:shots], rest[shots:]

    def late(layer):
        return add(*[packet[layer_rows(layer, size_y)] for packet in lates])

    size_y = speeds.shape[1]
    own = [own_out[layer_rows(i, size_y)] for i in range(2 * REACH)]
    parity = lax.rem(lax.axis_index("shot"), 2)
    for at in range(REACH):
        mine, number = parity == at // EARLY_SPEEDS, at % EARLY_SPEEDS
        speed = jnp.where(mine, shared[number], passed[number])
        next_mid[at], next_scaled[at] = next_halo(at, speed, late, own, points_out)
    for at in range(REACH):
        ahead = after[at] + across(at, lambda i: next_mid[i])
        back = after[REACH + at] + across(at, lambda i: next_scaled[i])
        speed = speeds[at]
        gradient[at] = 2.0 * speed * (back * outer[at] + outer[REACH + at] * ahead)
    scatter_rows(gradient, outputs, shots, False)


def add_kernel(*refs):
    refs[-1][...] = functools.reduce(lambda a, b: a + b, [ref[...] for ref in refs[:-1]])


def sum_kernel(inner, inner_near, *refs):
    outers, out = refs[:-1], refs[-1]
    odd = lax.rem(lax.axis_index("space"), 2)
    for at in range(REACH):
        out[placed(at, True, odd)] = functools.reduce(lambda a, b: a + b, [r[at] for r in outers])
        out[placed(at, False, odd)] = inner[at] + inner_near[at]


def call(kernel, shapes, in_spaces, scratch, flops, moved):
    def shape(given):
        return jax.ShapeDtypeStruct(given, F32) if isinstance(given, tuple) else given

    many = isinstance(shapes, list)
    return pl.pallas_call(
        kernel,
        out_shape=[shape(s) for s in shapes] if many else shape(shapes),
        in_specs=[pl.BlockSpec(memory_space=space) for space in in_spaces],
        out_specs=[pl.BlockSpec(memory_space=pltpu.VMEM) for _ in shapes]
        if many
        else pl.BlockSpec(memory_space=pltpu.VMEM),
        scratch_shapes=scratch,
        compiler_params=pltpu.CompilerParams(vmem_limit_bytes=VMEM_LIMIT),
        cost_estimate=pl.CostEstimate(flops=flops, bytes_accessed=moved, transcendentals=0),
    )


def both_ways(pairs):
    return pairs + [(b, a) for a, b in pairs]


def on_device(
    courant,
    field_old,
    field_now,
    adjoint_late,
    adjoint_now,
    source_x,
    source_yz,
    wavelet,
    receiver_x,
    receiver_yz,
    residual_trace,
):
    slab, size_y, size_z = courant.shape
    shots = lax.axis_size("shot")
    if slab != 2 * REACH or shots % 2:
        raise ValueError("unsupported slab")
    devices = lax.axis_size("space")
    plane = size_y * size_z
    part_rows = size_y // shots
    V, H = pltpu.VMEM, pltpu.HBM

    def stack(layers):
        return (layers, size_y, size_z)

    def held(layers):
        return pltpu.VMEM(stack(layers), F32)

    def in_hbm(values):
        return pltpu.with_memory_space_constraint(values, pltpu.HBM)

    out_pairs = both_ways([(i, i + 1) for i in range(1, devices - 1, 2)])
    in_pairs = [(i, i ^ 1) for i in range(devices)]
    relayed = devices == 8
    old, now, late, adjoint = (
        field[0] for field in (field_old, field_now, adjoint_late, adjoint_now)
    )
    place = [source_x.astype(F32), source_yz.astype(F32)]
    pulse = jnp.concatenate([wavelet[0]] + place).reshape(1, 4)

    early_layers = 2 * REACH + EARLY_SPEEDS
    early_out = call(
        early_kernel,
        (early_layers * size_y + EARLY_EXTRA, size_z),
        [H] * 3,
        [held(REACH)] * 3 + [pltpu.SemaphoreType.DMA((3,))],
        SMALL,
        SMALL,
    )(in_hbm(courant), in_hbm(now), in_hbm(adjoint))
    halo_out = lax.ppermute(early_out, "space", out_pairs)

    bands = jax.ShapeDtypeStruct((2, size_z, size_z), BF16)
    accel, adjoint_mid, speeds, adjoint_half, bands, early_in, late_out, late_in = call(
        local_kernel,
        [stack(slab)] * 4
        + [bands, stack(2 * REACH + INNER_SPEEDS)]
        + [(2 * REACH * size_y, size_z)]
        + [stack(3 * REACH - INNER_SPEEDS)],
        [pl.ANY] + [V] * 4 + [H],
        [held(slab)] * 3 + [pltpu.SemaphoreType.DMA(())],
        LARGE,
        SMALL,
    )(early_out, courant, now, adjoint, old, in_hbm(late))
    halo_in = lax.ppermute(early_in, "space", in_pairs)
    halo_late_in = lax.ppermute(late_in, "space", in_pairs)
    if relayed:
        first_hop = lax.ppermute(late_out, "space", [(3, 7), (4, 0)])
        halo_lates = [lax.ppermute(late_out, "space", both_ways([(1, 2), (5, 6)]))]
    else:
        halo_lates = [lax.ppermute(late_out, "space", out_pairs)]
    inner, outer_part, forward, backward, points_out = call(
        inner_kernel,
        [stack(2 * REACH), stack(3 * REACH)] + [stack(2 * REACH)] * 3,
        [V] * 14,
        [
            pltpu.VMEM((2 * slab * size_y, receiver_x.shape[1]), BF16),
            held(3 * slab),
            held(2 * REACH),
        ]
        + [held(REACH)] * 4,
        SMALL,
        SMALL,
    )(
        pulse,
        receiver_x,
        receiver_yz,
        residual_trace[0].T,
        early_in,
        speeds,
        accel,
        adjoint_mid,
        late_in,
        late_out,
        adjoint_half,
        bands,
        halo_in,
        halo_late_in,
    )
    if relayed:
        first_hop, inner = lax.optimization_barrier((first_hop, inner))
        halo_lates.append(lax.ppermute(first_hop, "space", [(7, 4), (0, 3)]))
    outer, step, shared, *inner_parts = call(
        functools.partial(middle_kernel, shots),
        [stack(2 * REACH)] * 2 + [stack(EARLY_SPEEDS)] + [(REACH, part_rows, size_z)] * shots,
        [V] * 6,
        [held(REACH)],
        MIDDLE_COST,
        SMALL,
    )(speeds, halo_out, inner, outer_part, forward, backward)
    after = call(second_kernel, stack(2 * REACH), [V] * 5, [], SECOND_COST, SMALL)(
        bands, outer, step, forward, backward
    )
    passed = lax.ppermute(
        lax.slice_in_dim(halo_out, 2 * REACH * size_y, early_layers * size_y).reshape(
            stack(EARLY_SPEEDS)
        ),
        "shot",
        [(i, i ^ 1) for i in range(shots)],
    )

    def exchanged(part, shift):
        return lax.ppermute(part, "shot", [(i, i ^ shift) for i in range(shots)])

    order = exchange_order(shots, True)
    inner_near = inner_parts[order.index(1)]
    early_parts = [
        exchanged(part, shift) if shift else part
        for part, shift in zip(inner_parts, order)
        if shift != 1
    ]
    inner_sum = call(
        add_kernel, (REACH, part_rows, size_z), [V] * (shots - 1), [], LARGE, SMALL
    )(*early_parts)
    order = exchange_order(shots, False)
    outer_parts = call(
        functools.partial(outer_kernel, shots, relayed),
        [(REACH, part_rows, size_z)] * shots,
        [V] * (7 + len(halo_lates)),
        [held(REACH)] * 3,
        SMALL,
        SMALL,
    )(early_out, speeds, outer, after, shared, passed, points_out, *halo_lates)
    inner_near, *outer_parts = lax.optimization_barrier((inner_near, *outer_parts))
    inner_near = exchanged(inner_near, 1)
    outer_parts = [
        exchanged(part, shift) if shift else part for part, shift in zip(outer_parts, order)
    ]
    return call(
        sum_kernel,
        (slab, part_rows, size_z),
        [V] * (2 + shots),
        [],
        SMALL,
        SMALL,
    )(inner_sum, inner_near, *outer_parts)


def solution(mesh):
    field = P("shot", "space", None, None)
    specs = (
        P("space", None, None),
        field,
        field,
        field,
        field,
        P("shot"),
        P("shot"),
        P("shot", None),
        P("shot", None),
        P("shot", None),
        P("shot", None, None),
    )
    return jax.shard_map(
        on_device, mesh=mesh, in_specs=specs, out_specs=P("space", "shot", None), check_vma=False
    )
```

```python
import functools
import jax
import jax.numpy as jnp
from jax import lax
from jax.experimental import pallas as pl
from jax.experimental.pallas import tpu as pltpu
from jax.sharding import PartitionSpec as P

MIDDLE = 3.0 * (-205.0 / 72.0)
SIDE = (8.0 / 5.0, -1.0 / 5.0, 8.0 / 315.0, -1.0 / 560.0)
REACH = 4
SCALE = 5040.0
WHOLE_SIDE = (8064.0, -1008.0, 128.0, -9.0)
EARLY_SPEEDS, INNER_SPEEDS = REACH // 2, REACH // 2
EARLY_EXTRA = 8
INWARD_ORDER, OUTWARD_ORDER = [2, 3, 1], [2, 3, 1]
F32 = jnp.float32
BF16 = jnp.bfloat16
VMEM_LIMIT = 32 * 1024 * 1024
MIDDLE_COST = int(8 * 10**9)
SECOND_COST = int(0.001 * 10**9)
SMALL, LARGE = 10**6, 10**10


def placed(layer, outward, odd):
    layer = layer if outward else 2 * REACH - 1 - layer
    return layer + odd * (2 * REACH - 1 - 2 * layer)


def grids(size_y, size_z):
    rows = lax.broadcasted_iota(jnp.int32, (size_y, size_z), 0)
    columns = lax.broadcasted_iota(jnp.int32, (size_y, size_z), 1)
    return rows, columns


def three_parts(values):
    high = values.astype(BF16)
    rest = values - high.astype(F32)
    middle = rest.astype(BF16)
    return high, middle, (rest - middle.astype(F32)).astype(BF16)


def band(size, block):
    rows, columns = grids(size, size)
    distance = jnp.abs(rows - columns)
    weights = jnp.zeros((size, size), F32)
    for offset in range(1, REACH + 1):
        weights = jnp.where(distance == offset, WHOLE_SIDE[offset - 1], weights)
    bits = block.bit_length() - 1
    same = jnp.right_shift(rows, bits) == jnp.right_shift(columns, bits)
    return jnp.where(same, weights, 0.0).astype(BF16)


def plane_laplace(layers, along_y, along_z):
    shape = (len(layers),) + layers[0].shape
    values = jnp.concatenate(layers, axis=0)
    total = None
    for part in three_parts(values)[::-1]:
        term = jnp.dot(part, along_z, preferred_element_type=F32)
        term += jnp.dot(along_y, part, preferred_element_type=F32)
        total = term if total is None else total + term
    return (total * (1.0 / SCALE) + MIDDLE * values).reshape(shape)


def weighted(terms):
    total = None
    for distance in range(1, REACH + 1):
        found = [layer() for at, layer in terms if at == distance]
        if found:
            term = SIDE[distance - 1] * functools.reduce(lambda a, b: a + b, found)
            total = term if total is None else total + term
    return total


def within(at, layers):
    return weighted([(abs(at - i), lambda i=i: layers(i)) for i in range(REACH) if i != at])


def from_other(at, layers):
    last = 2 * REACH - 1
    return weighted([(last - i - at, lambda i=i: layers(i)) for i in range(REACH)])


def across(at, layers):
    return weighted([(at + 1 + i, lambda i=i: layers(i)) for i in range(REACH)])


def add(*values):
    return functools.reduce(lambda a, b: a + b, [v for v in values if v is not None])


def layer_rows(layer, size_y):
    return slice(layer * size_y, (layer + 1) * size_y)


def early_kernel(courant, now, adjoint, packet, speeds, fields, adjoints, sems):
    size_y = fields.shape[1]
    odd = lax.rem(lax.axis_index("space"), 2)
    pairs = ((courant, speeds), (adjoint, adjoints), (now, fields))
    copies = [
        pltpu.make_async_copy(source.at[pl.ds(odd * REACH, REACH)], target, sems.at[number])
        for number, (source, target) in enumerate(pairs)
    ]
    for copy in copies:
        copy.start()
    for copy in copies:
        copy.wait()
    for layer in range(REACH):
        at = layer + odd * (REACH - 1 - 2 * layer)
        speed = speeds[at]
        packet[layer_rows(layer, size_y)] = fields[at]
        packet[layer_rows(REACH + layer, size_y)] = speed * speed * adjoints[at]
    parity = lax.rem(lax.axis_index("shot"), 2)
    for number in range(EARLY_SPEEDS):
        layer = parity * EARLY_SPEEDS + number
        at = layer + odd * (REACH - 1 - 2 * layer)
        packet[layer_rows(2 * REACH + number, size_y)] = speeds[at]
    packet[(2 * REACH + EARLY_SPEEDS) * size_y :, :] = fields[0, 0:EARLY_EXTRA, :]


def local_kernel(
    sent_first,
    courant,
    now,
    adjoint,
    old,
    late,
    accel,
    adjoint_mid,
    speeds,
    adjoint_now,
    bands,
    early_in,
    late_out,
    late_in,
    present,
    scaled,
    late_held,
    sem,
):
    size_y, size_z = courant.shape[1:]
    odd = lax.rem(lax.axis_index("space"), 2)
    copy = pltpu.make_async_copy(late, late_held, sem)
    copy.start()
    along_y, along_z = band(REACH * size_y, size_y), band(size_z, size_z)
    bands[0] = along_y
    bands[1] = along_z
    places = [placed(layer, half == 0, odd) for half in range(2) for layer in range(REACH)]
    for at, place in enumerate(places):
        speed = courant[place]
        speeds[at] = speed
        adjoint_now[at] = adjoint[place]
        present[at] = now[place]
        scaled[at] = speed * speed * adjoint[place]
    def put_out(layer, value):
        late_out[layer_rows(layer, size_y)] = value

    def put_in(layer, value):
        late_in[layer] = value

    for mine, put in ((0, put_out), (REACH, put_in)):
        other = REACH - mine
        flat = [
            plane_laplace([layers[mine + at] for at in range(REACH)], along_y, along_z)
            for layers in (present, scaled)
        ]
        if mine == 0:
            copy.wait()
        for at in range(REACH):
            place = places[mine + at]
            speed_sq = speeds[mine + at] * speeds[mine + at]
            laplace = add(
                flat[0][at],
                within(at, lambda i: present[mine + i]),
                from_other(at, lambda i: present[other + i]),
            )
            accel[mine + at] = laplace
            put(at, 2.0 * now[place] - old[place] + speed_sq * laplace)
            laplace = add(
                flat[1][at],
                within(at, lambda i: scaled[mine + i]),
                from_other(at, lambda i: scaled[other + i]),
            )
            field = 2.0 * adjoint[place] - late_held[place] + laplace
            adjoint_mid[mine + at] = field
            put(REACH + at, speed_sq * field)
    for layer in range(REACH):
        early_in[layer] = present[REACH + layer]
        early_in[REACH + layer] = scaled[REACH + layer]
        if layer < INNER_SPEEDS:
            early_in[2 * REACH + layer] = speeds[REACH + layer]
        else:
            late_in[2 * REACH + layer - INNER_SPEEDS] = speeds[REACH + layer]


def next_halo(at, speed, late, own, points):
    speed_sq = speed * speed
    mid = late(at) + speed_sq * (across(at, lambda i: own[i]) + points[at])
    scaled = late(REACH + at) + speed_sq * (
        across(at, lambda i: own[REACH + i]) + points[REACH + at]
    )
    return mid, scaled


def exchange_order(shots, inward):
    if shots == 4:
        return [0] + (INWARD_ORDER if inward else OUTWARD_ORDER)
    return list(range(shots))


def scatter_rows(gradient, outputs, shots, inward):
    rows = gradient.shape[1] // shots
    me = lax.axis_index("shot")
    for number, shift in enumerate(exchange_order(shots, inward)):
        first = pl.multiple_of(jnp.bitwise_xor(me, shift) * rows, rows)
        outputs[number][...] = gradient[:, pl.ds(first, rows), :]


def inner_kernel(
    pulse,
    receiver_x,
    receiver_yz,
    residual,
    own_in,
    speeds,
    accel,
    adjoint_mid,
    late_in,
    late_out,
    adjoint_now,
    bands,
    halo_early,
    halo_late,
    inner,
    outer,
    forward,
    backward,
    points_out,
    marks,
    added,
    points_in,
    mid,
    scaled,
    next_mid,
    next_scaled,
):
    slab = 2 * REACH
    space = lax.axis_index("space")
    odd = lax.rem(space, 2)
    size_y, size_z = own_in.shape[1:]
    along_y, along_z = bands[0], bands[1]
    z_bits = size_z.bit_length() - 1

    def counted(x):
        local = x - space * slab
        return REACH + local + odd * (slab - 1 - 2 * local)

    cells = receiver_yz[...]
    layer = counted(receiver_x[...])
    inside = (layer >= 0) & (layer < 2 * slab)
    wanted = jnp.where(inside, layer * size_y + jnp.right_shift(cells, z_bits), -1)
    count = wanted.shape[1]
    line = lax.broadcasted_iota(jnp.int32, (2 * slab * size_y, count), 0)
    marks[...] = jnp.where(line == wanted, 1.0, 0.0).astype(BF16)
    depth = lax.broadcasted_iota(jnp.int32, (size_z, count), 0)
    hit = depth == jnp.bitwise_and(cells, size_z - 1)

    def received(step, first, last):
        total = None
        for part in three_parts(residual[pl.ds(step, 1), :]):
            spread = jnp.where(hit, part.astype(F32), 0.0).astype(BF16)
            term = lax.dot_general(
                marks[first * size_y : last * size_y],
                spread,
                (((1,), (1,)), ((), ())),
                preferred_element_type=F32,
            )
            total = term if total is None else total + term
        return total.reshape(last - first, size_y, size_z)

    added[0 : 2 * slab] = received(0, 0, 2 * slab)
    added[2 * slab :] = received(1, REACH, REACH + slab)

    rows, columns = grids(size_y, size_z)
    cell = rows * size_z + columns
    source_layer = counted(pulse[:, 2:3].astype(jnp.int32))
    source_cell = pulse[:, 3:4].astype(jnp.int32)

    def fired(step, at):
        spot = jnp.where(source_layer == at, source_cell, -1)
        return jnp.where(cell == spot, pulse[:, step : step + 1], 0.0)

    for at in range(REACH):
        points_out[at] = fired(0, REACH - 1 - at)
        points_out[REACH + at] = added[REACH - 1 - at]
        points_in[at] = fired(0, REACH + slab + at)
        points_in[REACH + at] = added[REACH + slab + at]
        speed = speeds[at]
        fire = fired(0, REACH + at)
        outer[at] = accel[at] + fire
        outer[REACH + at] = adjoint_mid[at] + added[REACH + at]
        outer[2 * REACH + at] = late_out[layer_rows(at, size_y)] + speed * speed * fire
    for at in range(REACH):
        if at < INNER_SPEEDS:
            speed = halo_early[2 * REACH + at]
        else:
            speed = halo_late[2 * REACH + at - INNER_SPEEDS]
        next_mid[at], next_scaled[at] = next_halo(
            at, speed, lambda i: halo_late[i], own_in, points_in
        )
    for at in range(REACH):
        to = REACH + slab - 1 - at
        speed = speeds[REACH + at]
        speed_sq = speed * speed
        extra = across(at, lambda i: halo_early[i]) + fired(0, to)
        adjoint = adjoint_mid[REACH + at] + across(at, lambda i: halo_early[REACH + i]) + added[to]
        inner[at] = accel[REACH + at] + extra
        inner[REACH + at] = adjoint
        mid[at] = late_in[at] + speed_sq * extra
        scaled[at] = speed_sq * adjoint
    flat_mid = plane_laplace([mid[at] for at in range(REACH)], along_y, along_z)
    flat_scaled = plane_laplace([scaled[at] for at in range(REACH)], along_y, along_z)
    for at in range(REACH):
        to = REACH + at
        forward[at] = add(fired(1, to), from_other(at, lambda i: mid[i]))
        backward[at] = add(
            added[2 * slab + at] - adjoint_now[at],
            from_other(at, lambda i: scaled[i]),
        )
        to = REACH + slab - 1 - at
        forward[REACH + at] = add(
            flat_mid[at],
            fired(1, to),
            within(at, lambda i: mid[i]),
            across(at, lambda i: next_mid[i]),
        )
        backward[REACH + at] = add(
            flat_scaled[at],
            added[2 * slab + slab - 1 - at] - adjoint_now[REACH + at],
            2.0 * inner[REACH + at],
            within(at, lambda i: scaled[i]),
            across(at, lambda i: next_scaled[i]),
        )


def middle_kernel(shots, speeds, halo, inner, outer_part, forward, backward, outer, step, *rest):
    outputs, (gradient,) = rest[:shots], rest[shots:]
    size_y = speeds.shape[1]
    for at in range(REACH):
        speed = speeds[at]
        speed_sq = speed * speed
        extra = across(at, lambda i: halo[layer_rows(i, size_y)])
        adjoint = outer_part[REACH + at] + across(at, lambda i: halo[layer_rows(REACH + i, size_y)])
        outer[at] = outer_part[at] + extra
        outer[REACH + at] = adjoint
        step[at] = outer_part[2 * REACH + at] + speed_sq * extra
        step[REACH + at] = speed_sq * adjoint
    for at in range(REACH):
        ahead = add(forward[REACH + at], from_other(at, lambda i: step[i]))
        back = add(backward[REACH + at], from_other(at, lambda i: step[REACH + i]))
        speed = speeds[REACH + at]
        gradient[at] = 2.0 * speed * (back * inner[at] + inner[REACH + at] * ahead)
    scatter_rows(gradient, outputs, shots, True)


def second_kernel(bands, outer, step, forward, backward, after):
    along_y, along_z = bands[0], bands[1]
    flat_mid = plane_laplace([step[at] for at in range(REACH)], along_y, along_z)
    flat_scaled = plane_laplace([step[REACH + at] for at in range(REACH)], along_y, along_z)
    for at in range(REACH):
        after[at] = add(forward[at], flat_mid[at], within(at, lambda i: step[i]))
        after[REACH + at] = add(
            backward[at],
            2.0 * outer[REACH + at],
            flat_scaled[at],
            within(at, lambda i: step[REACH + i]),
        )


def outer_kernel(
    shots, relayed, own_out, speeds, outer, after, halo, passed, points_out, *rest
):
    lates, rest = rest[: 1 + relayed], rest[1 + relayed :]
    outputs, (next_mid, next_scaled, gradient) = rest[:shots], rest[shots:]

    def late(layer):
        return add(*[packet[layer_rows(layer, size_y)] for packet in lates])

    size_y = speeds.shape[1]
    own = [own_out[layer_rows(i, size_y)] for i in range(2 * REACH)]
    parity = lax.rem(lax.axis_index("shot"), 2)
    for at in range(REACH):
        mine, number = parity == at // EARLY_SPEEDS, at % EARLY_SPEEDS
        arrived = halo[layer_rows(2 * REACH + number, size_y)]
        speed = jnp.where(mine, arrived, passed[number])
        next_mid[at], next_scaled[at] = next_halo(at, speed, late, own, points_out)
    for at in range(REACH):
        ahead = after[at] + across(at, lambda i: next_mid[i])
        back = after[REACH + at] + across(at, lambda i: next_scaled[i])
        speed = speeds[at]
        gradient[at] = 2.0 * speed * (back * outer[at] + outer[REACH + at] * ahead)
    scatter_rows(gradient, outputs, shots, False)


def add_kernel(*refs):
    refs[-1][...] = functools.reduce(lambda a, b: a + b, [ref[...] for ref in refs[:-1]])


def sum_kernel(inner, inner_near, *refs):
    outers, out = refs[:-1], refs[-1]
    odd = lax.rem(lax.axis_index("space"), 2)
    for at in range(REACH):
        out[placed(at, True, odd)] = functools.reduce(lambda a, b: a + b, [r[at] for r in outers])
        out[placed(at, False, odd)] = inner[at] + inner_near[at]


def call(kernel, shapes, in_spaces, scratch, flops, moved):
    def shape(given):
        return jax.ShapeDtypeStruct(given, F32) if isinstance(given, tuple) else given

    many = isinstance(shapes, list)
    return pl.pallas_call(
        kernel,
        out_shape=[shape(s) for s in shapes] if many else shape(shapes),
        in_specs=[pl.BlockSpec(memory_space=space) for space in in_spaces],
        out_specs=[pl.BlockSpec(memory_space=pltpu.VMEM) for _ in shapes]
        if many
        else pl.BlockSpec(memory_space=pltpu.VMEM),
        scratch_shapes=scratch,
        compiler_params=pltpu.CompilerParams(vmem_limit_bytes=VMEM_LIMIT),
        cost_estimate=pl.CostEstimate(flops=flops, bytes_accessed=moved, transcendentals=0),
    )


def both_ways(pairs):
    return pairs + [(b, a) for a, b in pairs]


def on_device(
    courant,
    field_old,
    field_now,
    adjoint_late,
    adjoint_now,
    source_x,
    source_yz,
    wavelet,
    receiver_x,
    receiver_yz,
    residual_trace,
):
    slab, size_y, size_z = courant.shape
    shots = lax.axis_size("shot")
    if slab != 2 * REACH or shots % 2:
        raise ValueError("unsupported slab")
    devices = lax.axis_size("space")
    plane = size_y * size_z
    part_rows = size_y // shots
    V, H = pltpu.VMEM, pltpu.HBM

    def stack(layers):
        return (layers, size_y, size_z)

    def held(layers):
        return pltpu.VMEM(stack(layers), F32)

    def in_hbm(values):
        return pltpu.with_memory_space_constraint(values, pltpu.HBM)

    out_pairs = both_ways([(i, i + 1) for i in range(1, devices - 1, 2)])
    in_pairs = [(i, i ^ 1) for i in range(devices)]
    relayed = devices == 8
    old, now, late, adjoint = (
        field[0] for field in (field_old, field_now, adjoint_late, adjoint_now)
    )
    place = [source_x.astype(F32), source_yz.astype(F32)]
    pulse = jnp.concatenate([wavelet[0]] + place).reshape(1, 4)

    early_layers = 2 * REACH + EARLY_SPEEDS
    early_out = call(
        early_kernel,
        (early_layers * size_y + EARLY_EXTRA, size_z),
        [H] * 3,
        [held(REACH)] * 3 + [pltpu.SemaphoreType.DMA((3,))],
        SMALL,
        SMALL,
    )(in_hbm(courant), in_hbm(now), in_hbm(adjoint))
    halo_out = lax.ppermute(early_out, "space", out_pairs)

    bands = jax.ShapeDtypeStruct((2, size_z, size_z), BF16)
    accel, adjoint_mid, speeds, adjoint_half, bands, early_in, late_out, late_in = call(
        local_kernel,
        [stack(slab)] * 4
        + [bands, stack(2 * REACH + INNER_SPEEDS)]
        + [(2 * REACH * size_y, size_z)]
        + [stack(3 * REACH - INNER_SPEEDS)],
        [pl.ANY] + [V] * 4 + [H],
        [held(slab)] * 3 + [pltpu.SemaphoreType.DMA(())],
        LARGE,
        SMALL,
    )(early_out, courant, now, adjoint, old, in_hbm(late))
    halo_in = lax.ppermute(early_in, "space", in_pairs)
    halo_late_in = lax.ppermute(late_in, "space", in_pairs)
    if relayed:
        first_hop = lax.ppermute(late_out, "space", [(3, 7), (4, 0)])
        halo_lates = [lax.ppermute(late_out, "space", both_ways([(1, 2), (5, 6)]))]
    else:
        halo_lates = [lax.ppermute(late_out, "space", out_pairs)]
    inner, outer_part, forward, backward, points_out = call(
        inner_kernel,
        [stack(2 * REACH), stack(3 * REACH)] + [stack(2 * REACH)] * 3,
        [V] * 14,
        [
            pltpu.VMEM((2 * slab * size_y, receiver_x.shape[1]), BF16),
            held(3 * slab),
            held(2 * REACH),
        ]
        + [held(REACH)] * 4,
        SMALL,
        SMALL,
    )(
        pulse,
        receiver_x,
        receiver_yz,
        residual_trace[0].T,
        early_in,
        speeds,
        accel,
        adjoint_mid,
        late_in,
        late_out,
        adjoint_half,
        bands,
        halo_in,
        halo_late_in,
    )
    if relayed:
        first_hop, inner = lax.optimization_barrier((first_hop, inner))
        halo_lates.append(lax.ppermute(first_hop, "space", [(7, 4), (0, 3)]))
    outer, step, *inner_parts = call(
        functools.partial(middle_kernel, shots),
        [stack(2 * REACH)] * 2 + [(REACH, part_rows, size_z)] * shots,
        [V] * 6,
        [held(REACH)],
        MIDDLE_COST,
        SMALL,
    )(speeds, halo_out, inner, outer_part, forward, backward)
    after = call(second_kernel, stack(2 * REACH), [V] * 5, [], SECOND_COST, SMALL)(
        bands, outer, step, forward, backward
    )
    passed = lax.ppermute(
        lax.slice_in_dim(halo_out, 2 * REACH * size_y, early_layers * size_y).reshape(
            stack(EARLY_SPEEDS)
        ),
        "shot",
        [(i, i ^ 1) for i in range(shots)],
    )

    def exchanged(part, shift):
        return lax.ppermute(part, "shot", [(i, i ^ shift) for i in range(shots)])

    order = exchange_order(shots, True)
    inner_near = inner_parts[order.index(1)]
    early_parts = [
        exchanged(part, shift) if shift else part
        for part, shift in zip(inner_parts, order)
        if shift != 1
    ]
    inner_sum = call(
        add_kernel, (REACH, part_rows, size_z), [V] * (shots - 1), [], LARGE, SMALL
    )(*early_parts)
    order = exchange_order(shots, False)
    outer_parts = call(
        functools.partial(outer_kernel, shots, relayed),
        [(REACH, part_rows, size_z)] * shots,
        [V] * (7 + len(halo_lates)),
        [held(REACH)] * 3,
        SMALL,
        SMALL,
    )(early_out, speeds, outer, after, halo_out, passed, points_out, *halo_lates)
    inner_near, *outer_parts = lax.optimization_barrier((inner_near, *outer_parts))
    inner_near = exchanged(inner_near, 1)
    outer_parts = [
        exchanged(part, shift) if shift else part for part, shift in zip(outer_parts, order)
    ]
    return call(
        sum_kernel,
        (slab, part_rows, size_z),
        [V] * (2 + shots),
        [],
        SMALL,
        SMALL,
    )(inner_sum, inner_near, *outer_parts)


def solution(mesh):
    field = P("shot", "space", None, None)
    specs = (
        P("space", None, None),
        field,
        field,
        field,
        field,
        P("shot"),
        P("shot"),
        P("shot", None),
        P("shot", None),
        P("shot", None),
        P("shot", None, None),
    )
    return jax.shard_map(
        on_device, mesh=mesh, in_specs=specs, out_specs=P("space", "shot", None), check_vma=False
    )
```
